128 devices in a mesh: tile: 16 (over z_lo, x, core), head: 8 (over y, z_hi).
Axes of the slice: x: 4, y: 4, z: 4 (z_hi: 2, z_lo: 2; z = z_hi * 2 + z_lo), core: 2. Of those that a mesh axis runs over, the one named last changes fastest.
Arguments:
- tokens: bfloat16 [4096, 3072], P('tile'), may hold values from -6 to 6
- cotangent: bfloat16 [4096, 3072], P('tile'), may hold values from -6 to 6
- qkv_weight: bfloat16 [3072, 3, 3072], P('tile', None, 'head'), may hold values from -0.109375 to 0.109375
- out_weight: bfloat16 [3072, 3072], P('tile', 'head'), may hold values from -1.75 to 1.75
- slab_of_device: int32 [16], replicated, may hold values from 0 to 15, as said below
- extents: int32 [16, 2], replicated, may hold values from 0 to 1
Outputs:
- output: bfloat16 [4096, 3072], P('tile', 'head')
- grad_tokens: bfloat16 [4096, 3072], P('tile', 'head')
- grad_qkv_weight: float32 [3072, 3, 3072], P('tile', None, 'head')
- grad_out_weight: float32 [3072, 3072], P('tile', 'head')
The draws below stay inside these ranges and needn't reach their ends.
Inputs may be any that keep to these rules, and one draw needn't show every extreme that they name: slab_of_device[i] equals (r + i) mod 16 for every i, or (r - i) mod 16 for every i, with one r.
All inputs are finite; a program needn't handle non-finite values.
Results may differ from the reference program's by a relative error of at most 0.025.
Values may be sent and summed in bfloat16 or wider, within the bound.
A program may use at most 128 MiB of HBM per device.

```python
import math
import jax
import jax.numpy as jnp
from jax import lax

D = 3072
HEADS = 24
HD = 128
TILE_H = 8
TILE_W = 8
WT = 4
HT = 4
SLABS = 16
SLAB = 256
TOKENS = 4096
TILES = 16
N_TILE = 16
N_HEAD = 8


def draw_slab_of_device(key, part):
    key = jax.random.fold_in(key, 11)
    start_key, turn_key = jax.random.split(key)
    rotation = jax.random.randint(start_key, (), 0, SLABS, dtype=jnp.int32)
    direction = 2 * jax.random.randint(turn_key, (), 0, 2, dtype=jnp.int32) - 1
    positions = jnp.arange(SLABS, dtype=jnp.int32)
    return ((rotation + direction * positions) % SLABS).astype(jnp.int32)


def with_ends(result, rng, low, largest):
    index_at = [jax.random.randint(jax.random.fold_in(rng, axis), (), 0, length) for axis, length in enumerate(result.shape)]
    main_axis = result.shape.index(max(result.shape))
    neighbour = index_at[:main_axis] + [(index_at[main_axis] + 1) % result.shape[main_axis]] + index_at[main_axis + 1:]
    return result.at[tuple(index_at)].set(low).at[tuple(neighbour)].set(largest)


def raised(entries, stream_key, source, target, parts, factor):
    owner, partner = [(jnp.arange(entries.shape[dim]) // (entries.shape[dim] // parts)).reshape([-1 if axis == dim else 1 for axis in range(entries.ndim)]) for dim in (source, target)]
    chosen = jax.random.permutation(stream_key, parts)[partner]
    strong = (owner == chosen) | (owner == (partner + parts // 2) % parts)
    return jnp.where(strong, factor * entries, entries)


def block_levels(rng, dims, pieces, least, top_value):
    gain, own = 1.0, jax.random.fold_in(rng, 6)
    for dim, shards_of in pieces:
        heights = jnp.exp(jax.random.uniform(jax.random.fold_in(own, dim), (shards_of,), jnp.float32, least / len(pieces), top_value / len(pieces)))
        gain = gain * jnp.repeat(heights, dims[dim] // shards_of).reshape([-1 if axis == dim else 1 for axis in range(len(dims))])
    return gain


def normal_values(rng, dims, width, limit, shards=(), kind=jnp.bfloat16):
    factor_of = block_levels(rng, dims, shards, -0.22, 0.18) if shards else 1.0
    array = jax.random.normal(rng, dims, jnp.float32) * width * factor_of
    return jnp.minimum(jnp.maximum(array, -limit), limit).astype(kind)


def heavy_noise(key, extent, spread, limit, cuts, heavy, held_as=jnp.bfloat16):
    values = spread * jax.random.normal(key, extent, jnp.float32)
    if cuts:
        values = values * block_levels(key, extent, cuts, -0.22, 0.18)
    return jnp.clip(raised(values, jax.random.fold_in(key, 3), *heavy), -limit, limit).astype(held_as)


def setup_inputs(seed: int = 0) -> dict:
    streams_of = jax.random.split(jax.random.key(seed), 7)
    tokens = heavy_noise(streams_of[0], (TOKENS, D), 1.0, 6.0, ((0, 16),), (0, 1, 16, 2.0))
    cotangent = heavy_noise(streams_of[1], (TOKENS, D), 1.0, 6.0, ((0, 16),), (0, 1, 16, 2.0))
    qkv_weight = normal_values(streams_of[2], (D, 3, D), D ** -0.5, 0.109375, ((0, 16), (2, 8)))
    out_weight = normal_values(streams_of[3], (D, D), (max(D // 256, 1)) ** -0.5, 1.75, ((0, 16), (1, 8)))
    slab_of_device = draw_slab_of_device(jax.random.fold_in(streams_of[6], 71), 0)
    extents = with_ends(jax.random.randint(streams_of[5], (TILES, 2), 0, 2), jax.random.fold_in(streams_of[5], 1), 0, 1).astype(jnp.int32)
    return dict(tokens=tokens, cotangent=cotangent, qkv_weight=qkv_weight, out_weight=out_weight, slab_of_device=slab_of_device, extents=extents)


epsilon = 1e-06

def rounded(value):
    low = lax.optimization_barrier(value.astype(jnp.bfloat16))
    return low.astype(jnp.float32)

def block_sums(left, right, factor):

    def add_block(running, block_pair):
        term = jnp.dot(block_pair[0], block_pair[1], preferred_element_type=jnp.float32) * factor
        return (running + rounded(term), None)
    start_sum = jnp.zeros((left.shape[1], right.shape[2]), jnp.float32)
    return lax.scan(add_block, start_sum, (left, right))[0]

def unit_back(grad_unit, scale_rows, unit):
    return scale_rows * (grad_unit - unit * lax.optimization_barrier(jnp.mean(grad_unit * unit, axis=-1, keepdims=True)))

def reference(tokens, cotangent, qkv_weight, out_weight, slab_of_device, extents):
    tile_tokens = TILE_H * TILE_W
    group_width = D // N_HEAD
    inv_root = 1.0 / math.sqrt(HD)
    row_index = jnp.arange(TOKENS, dtype=jnp.int32)
    row_slab = slab_of_device[row_index // SLAB].astype(jnp.int32)
    row_height = row_slab % HT
    row_width = row_index % SLAB // tile_tokens
    row_reach = extents[(row_height * WT + row_width).astype(jnp.int32)]
    allowed = (jnp.abs(row_height[:, None] - row_height[None, :]) <= row_reach[:, 0:1]) & (jnp.abs(row_width[:, None] - row_width[None, :]) <= row_reach[:, 1:2])
    proj = jnp.dot(tokens, qkv_weight.reshape(D, 3 * D), preferred_element_type=jnp.float32)
    proj = proj.reshape(TOKENS, 3, HEADS, HD)
    query_raw = proj[:, 0]
    key_raw = proj[:, 1]
    values = proj[:, 2].astype(jnp.bfloat16)
    query_scale = lax.rsqrt(lax.optimization_barrier(jnp.mean(query_raw * query_raw, axis=-1, keepdims=True)) + epsilon)
    key_scale = lax.rsqrt(lax.optimization_barrier(jnp.mean(key_raw * key_raw, axis=-1, keepdims=True)) + epsilon)
    query_unit = query_raw * query_scale
    key_unit = key_raw * key_scale
    query = query_unit.astype(jnp.bfloat16)
    key = key_unit.astype(jnp.bfloat16)
    query_heads = jnp.swapaxes(query, 0, 1)
    key_heads = jnp.swapaxes(key, 0, 1)
    value_heads = jnp.swapaxes(values, 0, 1)

    def exp_scores(query_h, key_h):
        scores = jnp.dot(query_h, key_h.T, preferred_element_type=jnp.float32) * inv_root
        return jnp.where(allowed, jnp.exp(scores), 0.0)

    def forward_head(head_parts):
        query_h, key_h, value_h = head_parts
        weights_exp = exp_scores(query_h, key_h)
        denominator = lax.optimization_barrier(jnp.sum(weights_exp, axis=1))
        numerator = jnp.dot(weights_exp.astype(jnp.bfloat16), value_h, preferred_element_type=jnp.float32)
        return (numerator / denominator[:, None], denominator)
    context_heads, denom_heads = lax.map(forward_head, (query_heads, key_heads, value_heads))
    context = jnp.swapaxes(context_heads, 0, 1)
    attended = context.astype(jnp.bfloat16).reshape(TOKENS, D)
    output = block_sums(jnp.swapaxes(attended.reshape(TOKENS, N_HEAD, group_width), 0, 1), jnp.transpose(out_weight.reshape(D, N_HEAD, group_width), (1, 2, 0)), 1.0).astype(jnp.bfloat16)
    grad_attended = jnp.dot(cotangent, out_weight, preferred_element_type=jnp.float32).astype(jnp.bfloat16)
    grad_out_weight = block_sums(jnp.transpose(cotangent.reshape(N_TILE, SLAB, D), (0, 2, 1)), attended.reshape(N_TILE, SLAB, D), 1.0)
    grad_heads = grad_attended.reshape(TOKENS, HEADS, HD)
    row_delta = lax.optimization_barrier(jnp.sum(grad_heads.astype(jnp.float32) * context, axis=-1))

    def backward_head(head_parts):
        query_h, key_h, value_h, grad_h, denom_row, delta_row = head_parts
        probs = exp_scores(query_h, key_h) / denom_row[:, None]
        grad_probs = jnp.dot(grad_h, value_h.T, preferred_element_type=jnp.float32)
        grad_scores = (probs * (grad_probs - delta_row[:, None])).astype(jnp.bfloat16)
        probs_low = probs.astype(jnp.bfloat16)
        grad_query_unit = jnp.dot(grad_scores, key_h, preferred_element_type=jnp.float32) * inv_root
        grad_key_unit = block_sums(jnp.transpose(grad_scores.reshape(N_TILE, SLAB, TOKENS), (0, 2, 1)), query_h.reshape(N_TILE, SLAB, HD), inv_root)
        grad_values = block_sums(jnp.transpose(probs_low.reshape(N_TILE, SLAB, TOKENS), (0, 2, 1)), grad_h.reshape(N_TILE, SLAB, HD), 1.0)
        return (grad_query_unit, grad_key_unit, grad_values)
    grads = lax.map(backward_head, (query_heads, key_heads, value_heads, jnp.swapaxes(grad_heads, 0, 1), denom_heads, jnp.swapaxes(row_delta, 0, 1)))
    grad_query_unit = jnp.swapaxes(grads[0], 0, 1)
    grad_key_unit = jnp.swapaxes(grads[1], 0, 1)
    grad_values = jnp.swapaxes(grads[2], 0, 1)
    grad_query = unit_back(grad_query_unit, query_scale, query_unit)
    grad_key = unit_back(grad_key_unit, key_scale, key_unit)
    grad_proj = jnp.stack([grad_query, grad_key, grad_values], axis=1).reshape(TOKENS, 3, D).astype(jnp.bfloat16)
    left_groups = jnp.transpose(grad_proj.reshape(TOKENS, 3, N_HEAD, group_width), (2, 0, 1, 3))
    right_groups = jnp.transpose(qkv_weight.reshape(D, 3, N_HEAD, group_width), (2, 1, 3, 0))
    grad_tokens = block_sums(left_groups.reshape(N_HEAD, TOKENS, 3 * group_width), right_groups.reshape(N_HEAD, 3 * group_width, D), 1.0).astype(jnp.bfloat16)
    grad_qkv_weight = block_sums(jnp.transpose(tokens.reshape(N_TILE, SLAB, D), (0, 2, 1)), grad_proj.reshape(N_TILE, SLAB, 3 * D), 1.0).reshape(D, 3, D)
    return (output, grad_tokens, grad_qkv_weight, grad_out_weight)
```

```python
import math

import jax
import jax.numpy as jnp
from jax import lax
from jax.experimental import pallas as pl
from jax.experimental.pallas import tpu as pltpu
from jax.sharding import PartitionSpec as P

MESH = pl.DeviceIdType.MESH
HD = 128
NH = 3
ROWS = 256
WID = NH * HD
D = 3072
OWN = 192
EPS = 1e-06
INV_ROOT = 1.0 / math.sqrt(HD)
EXP2_SCALE = INV_ROOT * math.log2(math.e)
BF = jnp.bfloat16
F32 = jnp.float32
GATHER_COPIES = 17
SCATTER_COPIES = 7


def dot(a, b):
    return jnp.dot(a, b, preferred_element_type=F32)


def dot_nt(a, b):
    return lax.dot_general(a, b, (((1,), (1,)), ((), ())), preferred_element_type=F32)


def at_tile(z, x, c):
    return z * 8 + x * 2 + c


class Place:
    def __init__(self):
        t = lax.axis_index("tile")
        self.me = t
        self.z, self.x, self.c = t // 8, (t // 2) % 4, t % 2
        self.xr, self.xl, self.xo = (self.x + 1) % 4, (self.x + 3) % 4, (self.x + 2) % 4
        self.right = at_tile(self.z, self.xr, self.c)
        self.left = at_tile(self.z, self.xl, self.c)
        self.across = at_tile(1 - self.z, self.x, self.c)
        self.sib = at_tile(self.z, self.x, 1 - self.c)


class Gather:
    def __init__(self, place, buf, send, recv):
        self.p, self.buf, self.send, self.recv = place, buf, send, recv
        self.half_rows = buf.shape[1] // 2
        self.sent = []

    def slot(self, t):
        return self.buf.at[t]

    def half(self, t, i):
        return self.buf.at[t, pl.ds(i * self.half_rows, self.half_rows)]

    def copy(self, k, ref, dev):
        return pltpu.make_async_remote_copy(
            src_ref=ref, dst_ref=ref, send_sem=self.send.at[k], recv_sem=self.recv.at[k],
            device_id={"tile": dev}, device_id_type=MESH)

    def go(self, k, ref, dev):
        c = self.copy(k, ref, dev)
        c.start()
        self.sent.append(c)

    def got(self, k, ref):
        self.copy(k, ref, self.p.sib).wait_recv()

    def start(self):
        p = self.p
        me = self.slot(p.me)
        self.go(0, me, p.right)
        self.go(1, me, p.left)
        self.go(2, me, p.across)
        self.go(3, me, p.sib)

    def step_across(self):
        p = self.p
        s = self.slot(p.across)
        self.got(2, s)
        self.go(4, s, p.right)
        self.go(5, s, p.left)
        self.go(6, s, p.sib)

    def step_sides(self):
        p = self.p
        for i, zz in enumerate((p.z, 1 - p.z)):
            tl, tr = at_tile(zz, p.xl, p.c), at_tile(zz, p.xr, p.c)
            self.got((0, 4)[i], self.slot(tl))
            self.go(7 + i, self.half(tl, 0), p.right)
            self.got((1, 5)[i], self.slot(tr))
            self.go(9 + i, self.half(tr, 1), p.left)
            self.go(11 + i, self.slot(tl), p.sib)
            self.go(13 + i, self.slot(tr), p.sib)

    def step_opposite(self):
        p = self.p
        for i, zz in enumerate((p.z, 1 - p.z)):
            to = at_tile(zz, p.xo, p.c)
            self.got(7 + i, self.half(to, 0))
            self.got(9 + i, self.half(to, 1))
            self.go(15 + i, self.slot(to), p.sib)

    def sib_own(self):
        p = self.p
        self.got(3, self.slot(p.sib))

    def sib_across(self):
        p = self.p
        self.got(6, self.slot(at_tile(1 - p.z, p.x, 1 - p.c)))

    def sib_sides(self):
        p = self.p
        for i, zz in enumerate((p.z, 1 - p.z)):
            self.got(11 + i, self.slot(at_tile(zz, p.xl, 1 - p.c)))
            self.got(13 + i, self.slot(at_tile(zz, p.xr, 1 - p.c)))

    def sib_opposite(self):
        p = self.p
        for i, zz in enumerate((p.z, 1 - p.z)):
            self.got(15 + i, self.slot(at_tile(zz, p.xo, 1 - p.c)))

    def finish(self):
        for c in self.sent:
            c.wait_send()


class Scatter:
    def __init__(self, axis, ring, pair, devices, parts, far, near, last, send, recv):
        self.axis, self.ring, self.pair = axis, ring, pair
        self.right, self.left, self.across = devices
        self.parts, self.far, self.near, self.last = parts, far, near, last
        self.send, self.recv = send, recv
        self.rr, self.rl, self.ro = (ring + 1) % 4, (ring + 3) % 4, (ring + 2) % 4
        rows = parts.shape[2]
        self.lo, self.hi = pl.ds(0, rows // 2), pl.ds(rows // 2, rows // 2)
        self.sent = []

    def copy(self, k, src, dst, dev):
        return pltpu.make_async_remote_copy(
            src_ref=src, dst_ref=dst, send_sem=self.send.at[k], recv_sem=self.recv.at[k],
            device_id={self.axis: dev}, device_id_type=MESH)

    def go(self, k, src, dst, dev):
        c = self.copy(k, src, dst, dev)
        c.start()
        self.sent.append(c)

    def got(self, k, dst):
        self.copy(k, dst, dst, self.right).wait_recv()

    def add(self, ring, rows, got):
        for i in range(2):
            self.parts[ring, i, rows] = (
                self.parts[ring, i, rows].astype(F32) + got[i].astype(F32)).astype(BF)

    def start_far(self):
        self.go(0, self.parts.at[self.ro, :, self.lo], self.far.at[0], self.right)
        self.go(1, self.parts.at[self.ro, :, self.hi], self.far.at[1], self.left)

    def start_near(self):
        self.go(2, self.parts.at[self.rr, :, self.hi], self.near.at[0, :, self.hi], self.right)
        self.go(3, self.parts.at[self.rl, :, self.lo], self.near.at[1, :, self.lo], self.left)

    def step_near(self):
        self.got(0, self.far.at[0])
        self.add(self.rr, self.lo, self.far.at[0])
        self.go(4, self.parts.at[self.rr, :, self.lo], self.near.at[0, :, self.lo], self.right)
        self.got(1, self.far.at[1])
        self.add(self.rl, self.hi, self.far.at[1])
        self.go(5, self.parts.at[self.rl, :, self.hi], self.near.at[1, :, self.hi], self.left)

    def total(self, pair):
        return (self.parts[self.ring, pair].astype(F32) + self.near[0, pair].astype(F32)
                + self.near[1, pair].astype(F32))

    def step_pair(self):
        self.got(2, self.near.at[0, :, self.hi])
        self.got(3, self.near.at[1, :, self.lo])
        self.got(4, self.near.at[0, :, self.lo])
        self.got(5, self.near.at[1, :, self.hi])
        other = 1 - self.pair
        self.parts[self.ring, other] = self.total(other).astype(BF)
        self.go(6, self.parts.at[self.ring, other], self.last, self.across)

    def result(self):
        self.got(6, self.last)
        return self.total(self.pair) + self.last[...].astype(F32)

    def finish(self):
        for c in self.sent:
            c.wait_send()


def kernel(tok_hbm, cot_hbm, w_hbm, wo_hbm, slab, ext,
           out_ref, gtok_ref, gqkv_ref, gout_ref,
           w, wo, kv, tok, cot, tok_t, tok_sib, cot_t, cot_sib, wexp, mask,
           proj, q, qt, g, gt, num, den, delta, dq, att, gp, dkv_sum,
           dkv_out, dkv_parts, dkv_far, dkv_near, dkv_last,
           gq_parts, gq_far, gq_near, gq_last,
           go_parts, go_far, go_near, go_last,
           hd_parts, ho_far, ho_near, ho_last, ht_far, ht_near, ht_last,
           load_sem, gat_send, gat_recv, sca_send, sca_recv, sib_send, sib_recv, dkv_send, dkv_recv):
    p = Place()
    hd = lax.axis_index("head")
    hy, hz = hd // 2, hd % 2
    head_devices = (((hy + 1) % 4) * 2 + hz, ((hy + 3) % 4) * 2 + hz, hy * 2 + 1 - hz)
    lane_devices = (p.right, p.left, p.across)

    loads = [pltpu.make_async_copy(a, b, load_sem.at[i]) for i, (a, b) in enumerate((
        (w_hbm, w.at[p.me]), (wo_hbm, wo.at[p.me]), (tok_hbm, tok), (cot_hbm, cot)))]
    for c in loads:
        c.start()

    barrier = pltpu.get_barrier_semaphore()
    for dev in (p.right, p.left, p.across, p.sib):
        pl.semaphore_signal(barrier, inc=1, device_id={"tile": dev}, device_id_type=MESH)
    for dev in head_devices:
        pl.semaphore_signal(barrier, inc=1, device_id={"head": dev}, device_id_type=MESH)
    pl.semaphore_wait(barrier, 7)

    sent = []

    def to_sibling(k, src, dst):
        c = pltpu.make_async_remote_copy(
            src_ref=src, dst_ref=dst, send_sem=sib_send.at[k], recv_sem=sib_recv.at[k],
            device_id={"tile": p.sib}, device_id_type=MESH)
        c.start()
        sent.append(c)
        return c

    gather_w = Gather(p, w, gat_send.at[0], gat_recv.at[0])
    gather_o = Gather(p, wo, gat_send.at[1], gat_recv.at[1])
    gather_kv = Gather(p, kv, gat_send.at[2], gat_recv.at[2])
    scatter = lambda i, parts, far, near, last: Scatter(
        "tile", p.x, p.z, lane_devices, parts, far, near, last, sca_send.at[i], sca_recv.at[i])
    head_scatter = lambda i, parts, far, near, last: Scatter(
        "head", hy, hz, head_devices, parts, far, near, last, sca_send.at[i], sca_recv.at[i])
    sum_dkv = scatter(0, dkv_parts, dkv_far, dkv_near, dkv_last)
    sum_gq = scatter(1, gq_parts, gq_far, gq_near, gq_last)
    sum_go = scatter(2, go_parts, go_far, go_near, go_last)
    sum_out = head_scatter(3, hd_parts, ho_far, ho_near, ho_last)
    sum_tok = head_scatter(4, hd_parts, ht_far, ht_near, ht_last)

    loads[0].wait()
    gather_w.start()

    height = lax.rem(slab[p.me], 4)
    near_height = lax.rem(slab[p.sib], 4)
    far_height = lax.rem(slab[at_tile(p.z, p.xr, 1 - p.c)], 4)
    key_width = lax.broadcasted_iota(jnp.int32, (64, ROWS), 1) // 64
    for qw in range(4):
        reach_h = ext[height * 4 + qw, 0]
        reach_w = ext[height * 4 + qw, 1]
        near_w = jnp.where(jnp.abs(key_width - qw) <= reach_w, 1.0, 0.0)
        for m, other in enumerate((height, near_height, far_height)):
            gap = jnp.full((64, ROWS), jnp.abs(height - other), jnp.int32)
            mask[m, qw * 64:(qw + 1) * 64] = jnp.where(gap <= reach_h, near_w, 0.0)

    loads[2].wait()
    loads[3].wait()

    def turn(src, dst):
        def body(j, carry):
            cols = pl.ds(pl.multiple_of(j * 384, 384), 384)
            dst[j] = src[:, cols].T.reshape(2, OWN, ROWS)
            return carry
        lax.fori_loop(0, 8, body, 0)

    turn(tok, tok_t)
    tok_swap = to_sibling(0, tok_t.at[:, 1 - p.c], tok_sib)

    def project(z, x, first=False):
        j = z * 4 + x
        t = tok[:, pl.ds(pl.multiple_of(j * 384, 384), 384)]
        for i in range(3):
            chunk = w[pl.ds(2 * j, 2), i * OWN:(i + 1) * OWN, :].reshape(2 * OWN, WID)
            if first:
                proj[i] = dot(t, chunk)
            else:
                proj[i] += dot(t, chunk)

    gather_w.step_across()
    turn(cot, cot_t)
    cot_swap = to_sibling(1, cot_t.at[:, 1 - p.c], cot_sib)
    gather_w.sib_own()
    project(p.z, p.x, True)
    gather_w.sib_across()
    project(1 - p.z, p.x)
    gather_w.step_sides()
    loads[1].wait()
    gather_o.start()
    gather_w.sib_sides()
    for zz in (p.z, 1 - p.z):
        project(zz, p.xl)
        project(zz, p.xr)
    gather_w.step_opposite()
    gather_o.step_across()
    gather_w.sib_opposite()
    for zz in (p.z, 1 - p.z):
        project(zz, p.xo)

    def scale_of(raw):
        return lax.rsqrt(jnp.mean(raw * raw, axis=-1, keepdims=True) + EPS)

    for h in range(NH):
        hs = slice(h * HD, (h + 1) * HD)
        raw = proj[1, :, hs]
        kv[p.me, :, hs] = (raw * scale_of(raw)).astype(BF)
    kv[p.me, :, WID:] = proj[2].astype(BF)
    gather_kv.start()
    for h in range(NH):
        hs = slice(h * HD, (h + 1) * HD)
        raw = proj[0, :, hs]
        unit = (raw * scale_of(raw)).astype(BF)
        q[:, hs] = unit
        qt[h] = unit.T

    def forward(t, m, i, first=False):
        for h in range(NH):
            hs = slice(h * HD, (h + 1) * HD)
            vs = slice(WID + h * HD, WID + (h + 1) * HD)
            scores = dot_nt(q[:, hs], kv[t, :, hs])
            we = jnp.exp2(scores * EXP2_SCALE) * mask[m]
            wexp[i, h] = we
            part = we[:, :HD] + we[:, HD:]
            val = dot(we.astype(BF), kv[t, :, vs])
            if first:
                den[h] = part
                num[:, hs] = val
            else:
                den[h] += part
                num[:, hs] += val

    def loop2(fn):
        lax.fori_loop(0, 2, lambda i, carry: (fn(i), carry)[1], 0)

    gather_o.step_sides()
    forward(p.me, 0, 0, True)
    gather_kv.step_across()
    gather_kv.sib_own()
    forward(p.sib, 1, 2)
    gather_o.step_opposite()
    forward(p.across, 0, 1)
    gather_kv.sib_across()
    forward(at_tile(1 - p.z, p.x, 1 - p.c), 1, 3)
    gather_o.sib_own()
    gather_o.sib_across()
    gather_o.sib_sides()
    gather_o.sib_opposite()

    def grad_att(j, acc):
        cols = pl.ds(pl.multiple_of(j * 384, 384), 384)
        return acc + dot(cot[:, cols], wo[pl.ds(2 * j, 2)].reshape(2 * OWN, WID))

    g[...] = lax.fori_loop(0, 8, grad_att, jnp.zeros((ROWS, WID), F32)).astype(BF)
    for h in range(NH):
        gt[h] = g[:, h * HD:(h + 1) * HD].T
    gather_kv.step_sides()
    gather_kv.sib_sides()

    def sides(i):
        zz = (p.z + i) % 2
        forward(at_tile(zz, p.xl, 1 - p.c), 2, 4 + 2 * i)
        forward(at_tile(zz, p.xr, 1 - p.c), 2, 5 + 2 * i)

    loop2(sides)
    gather_kv.step_opposite()
    loop2(lambda i: forward(at_tile((p.z + i) % 2, p.xo, p.c), 0, 8 + i))
    gather_kv.sib_opposite()
    loop2(lambda i: forward(at_tile((p.z + i) % 2, p.xo, 1 - p.c), 1, 10 + i))

    for h in range(NH):
        hs = slice(h * HD, (h + 1) * HD)
        inverse = 1.0 / jnp.sum(den[h], axis=-1, keepdims=True)
        context = num[:, hs] * inverse
        att[0, :, hs] = context.astype(BF)
        row = jnp.sum(g[:, hs].astype(F32) * context, axis=-1, keepdims=True)
        delta[h] = jnp.broadcast_to(row, (ROWS, HD))
        den[h] = jnp.broadcast_to(inverse, (ROWS, HD))
    att_swap = to_sibling(2, att.at[0], att.at[1])

    def backward(t, i, dst, first=False, adding=False):
        for h in range(NH):
            hs = slice(h * HD, (h + 1) * HD)
            vs = slice(WID + h * HD, WID + (h + 1) * HD)
            grad = dot_nt(g[:, hs], kv[t, :, vs])
            inverse, row = den[h], delta[h]
            probs, ds = [], []
            for part in range(2):
                cs = slice(part * HD, (part + 1) * HD)
                pr = wexp[i, h, :, cs] * inverse
                ds.append((pr * (grad[:, cs] - row)).astype(BF))
                probs.append(pr.astype(BF))
            probs = jnp.concatenate(probs, axis=1)
            ds = jnp.concatenate(ds, axis=1)
            term = dot(ds, kv[t, :, hs])
            if first:
                dq[:, hs] = term
            else:
                dq[:, hs] += term
            dk = dot(qt[h], ds) * INV_ROOT
            dv = dot(gt[h], probs)
            if adding:
                dk = dk + dst[hs].astype(F32)
                dv = dv + dst[vs].astype(F32)
            dst[hs] = dk.astype(BF)
            dst[vs] = dv.astype(BF)

    def swap_copy(x, z, k):
        return pltpu.make_async_remote_copy(
            src_ref=dkv_out.at[x, z], dst_ref=dkv_parts.at[x, z], send_sem=dkv_send.at[k],
            recv_sem=dkv_recv.at[k], device_id={"tile": p.sib}, device_id_type=MESH)

    def swap(x, z, k):
        c = swap_copy(x, z, k)
        c.start()
        sent.append(c)

    def out_part(j, carry):
        hd_parts[j // 2, j % 2] = dot_nt(att[0], wo[pl.ds(2 * j, 2)].reshape(2 * OWN, WID)).astype(BF)
        return carry

    def opposite_sib(i):
        zz = (p.z + i) % 2
        backward(at_tile(zz, p.xo, 1 - p.c), 10 + i, dkv_out.at[p.xo, zz])

    dq[...] = jnp.zeros_like(dq)
    loop2(opposite_sib)
    swap(p.xo, p.z, 0)
    swap(p.xo, 1 - p.z, 1)
    lax.fori_loop(0, 8, out_part, 0)
    sum_out.start_far()
    sum_out.start_near()

    def sides_sib(i):
        zz = (p.z + i) % 2
        backward(at_tile(zz, p.xl, 1 - p.c), 4 + 2 * i, dkv_out.at[p.xl, zz])
        backward(at_tile(zz, p.xr, 1 - p.c), 5 + 2 * i, dkv_out.at[p.xr, zz])

    loop2(sides_sib)
    for i, zz in enumerate((p.z, 1 - p.z)):
        swap(p.xl, zz, 2 + i)
        swap(p.xr, zz, 4 + i)
    for i, zz in enumerate((p.z, 1 - p.z)):
        swap_copy(p.xo, zz, i).wait_recv()

    def opposite_own(i):
        zz = (p.z + i) % 2
        backward(at_tile(zz, p.xo, p.c), 8 + i, dkv_parts.at[p.xo, zz], adding=True)

    loop2(opposite_own)
    sum_dkv.start_far()
    for i, zz in enumerate((p.z, 1 - p.z)):
        swap_copy(p.xl, zz, 2 + i).wait_recv()
        swap_copy(p.xr, zz, 4 + i).wait_recv()
    sum_dkv.start_near()

    def own_sib(i):
        zz = (p.z + i) % 2
        backward(at_tile(zz, p.x, 1 - p.c), 2 + i, dkv_out.at[p.x, zz])

    loop2(own_sib)
    for i, zz in enumerate((p.z, 1 - p.z)):
        swap(p.x, zz, 6 + i)
    sum_out.step_near()
    sum_dkv.step_near()
    for i, zz in enumerate((p.z, 1 - p.z)):
        swap_copy(p.x, zz, 6 + i).wait_recv()

    def own_own(i):
        zz = (p.z + i) % 2
        backward(at_tile(zz, p.x, p.c), i, dkv_parts.at[p.x, zz], adding=True)

    loop2(own_own)

    att_swap.wait_recv()
    cot_swap.wait_recv()

    def out_grad(j, carry):
        go_parts[j % 4, j // 4] = (dot(cot_t[j, p.c], att[0]) + dot(cot_sib[j], att[1])).astype(BF)
        return carry

    lax.fori_loop(0, 8, out_grad, 0)
    sum_go.start_far()
    sum_go.start_near()

    def unit_back(grad, raw):
        scale = scale_of(raw)
        unit = raw * scale
        return scale * (grad - unit * jnp.mean(grad * unit, axis=-1, keepdims=True))

    for h in range(NH):
        hs = slice(h * HD, (h + 1) * HD)
        gp[0, 0, :, hs] = unit_back(dq[:, hs] * INV_ROOT, proj[0, :, hs]).astype(BF)
    sum_out.step_pair()
    sum_dkv.step_pair()
    sum_go.step_near()
    out_ref[...] = sum_out.result().astype(BF)
    dkv_sum[...] = sum_dkv.result()
    for h in range(NH):
        hs = slice(h * HD, (h + 1) * HD)
        vs = slice(WID + h * HD, WID + (h + 1) * HD)
        gp[0, 1, :, hs] = unit_back(dkv_sum[hs].T, proj[1, :, hs]).astype(BF)
        gp[0, 2, :, hs] = dkv_sum[vs].T.astype(BF)
    gp_swap = to_sibling(3, gp.at[0], gp.at[1])
    sum_go.step_pair()

    tok_swap.wait_recv()
    gp_swap.wait_recv()

    def qkv_grad(j):
        for i in range(3):
            gq_parts[j % 4, j // 4, i * OWN:(i + 1) * OWN] = (
                dot(tok_t[j, p.c], gp[0, i]) + dot(tok_sib[j], gp[1, i])).astype(BF)

    loop2(lambda i: qkv_grad(i * 4 + p.xo))
    sum_gq.start_far()
    loop2(lambda i: qkv_grad(i * 4 + p.xr))
    loop2(lambda i: qkv_grad(i * 4 + p.xl))
    sum_gq.start_near()
    sum_out.finish()

    def tok_part(j, carry):
        acc = dot_nt(gp[0, 0], w[pl.ds(2 * j, 2), 0:OWN, :].reshape(2 * OWN, WID))
        for i in range(1, 3):
            acc += dot_nt(gp[0, i], w[pl.ds(2 * j, 2), i * OWN:(i + 1) * OWN, :].reshape(2 * OWN, WID))
        hd_parts[j // 2, j % 2] = acc.astype(BF)
        return carry

    lax.fori_loop(0, 8, tok_part, 0)
    sum_tok.start_far()
    sum_tok.start_near()
    loop2(lambda i: qkv_grad(i * 4 + p.x))
    sum_gq.step_near()
    sum_tok.step_near()
    gout_ref[...] = sum_go.result()
    sum_tok.step_pair()
    sum_gq.step_pair()
    gtok_ref[...] = sum_tok.result().astype(BF)
    gqkv_ref[...] = sum_gq.result()

    for s in (gather_w, gather_o, gather_kv, sum_dkv, sum_gq, sum_go, sum_tok):
        s.finish()
    for c in sent:
        c.wait_send()


def lane_bufs(rows, cols):
    return [pltpu.VMEM((2, 2, rows // 2, cols), BF), pltpu.VMEM((2, 2, rows, cols), BF),
            pltpu.VMEM((rows, cols), BF)]


def local(tokens, cotangent, qkv_weight, out_weight, slab_of_device, extents):
    w = jnp.transpose(qkv_weight, (1, 0, 2)).reshape(3 * OWN, WID)
    vm = lambda *shape, dtype=BF: pltpu.VMEM(shape, dtype)
    dma = lambda *shape: pltpu.SemaphoreType.DMA(shape)
    scratch = [
        vm(16, 3 * OWN, WID), vm(16, OWN, WID), vm(16, ROWS, 2 * WID), vm(ROWS, D), vm(ROWS, D),
        vm(8, 2, OWN, ROWS), vm(8, OWN, ROWS), vm(8, 2, OWN, ROWS), vm(8, OWN, ROWS),
        vm(12, NH, ROWS, ROWS, dtype=F32), vm(3, ROWS, ROWS, dtype=F32),
        vm(3, ROWS, WID, dtype=F32), vm(ROWS, WID), vm(NH, HD, ROWS), vm(ROWS, WID), vm(NH, HD, ROWS),
        vm(ROWS, WID, dtype=F32), vm(NH, ROWS, HD, dtype=F32), vm(NH, ROWS, HD, dtype=F32),
        vm(ROWS, WID, dtype=F32), vm(2, ROWS, WID), vm(2, 3, ROWS, WID), vm(2 * WID, ROWS, dtype=F32),
        vm(4, 2, 2 * WID, ROWS), vm(4, 2, 2 * WID, ROWS), *lane_bufs(2 * WID, ROWS),
        vm(4, 2, 3 * OWN, WID), *lane_bufs(3 * OWN, WID),
        vm(4, 2, OWN, WID), *lane_bufs(OWN, WID),
        vm(4, 2, ROWS, WID), *lane_bufs(ROWS, WID), *lane_bufs(ROWS, WID),
        dma(4), dma(3, GATHER_COPIES), dma(3, GATHER_COPIES), dma(5, SCATTER_COPIES), dma(5, SCATTER_COPIES),
        dma(4), dma(4), dma(8), dma(8),
    ]
    any_spec = pl.BlockSpec(memory_space=pl.ANY)
    smem = pl.BlockSpec(memory_space=pltpu.SMEM)
    vmem = pl.BlockSpec(memory_space=pltpu.VMEM)
    output, grad_tokens, grad_qkv, grad_out = pl.pallas_call(
        kernel,
        out_shape=(
            jax.ShapeDtypeStruct((ROWS, WID), BF), jax.ShapeDtypeStruct((ROWS, WID), BF),
            jax.ShapeDtypeStruct((3 * OWN, WID), F32), jax.ShapeDtypeStruct((OWN, WID), F32)),
        in_specs=[any_spec] * 4 + [smem] * 2,
        out_specs=(vmem,) * 4,
        scratch_shapes=scratch,
        compiler_params=pltpu.CompilerParams(
            collective_id=0, has_side_effects=True, vmem_limit_bytes=64 * 1024 * 1024),
        cost_estimate=pl.CostEstimate(flops=20_000_000_000, bytes_accessed=10_000_000, transcendentals=2_400_000),
        name="sublayer",
    )(tokens, cotangent, w, out_weight, slab_of_device, extents)
    grad_qkv = jnp.transpose(grad_qkv.reshape(3, OWN, WID), (1, 0, 2))
    return output, grad_tokens, grad_qkv, grad_out


def solution(mesh):
    return jax.shard_map(
        local, mesh=mesh,
        in_specs=(P("tile", None), P("tile", None), P("tile", None, "head"), P("tile", "head"), P(None), P(None, None)),
        out_specs=(P("tile", "head"), P("tile", "head"), P("tile", None, "head"), P("tile", "head")),
        check_vma=False)
```

```python
import math

import jax
import jax.numpy as jnp
from jax import lax
from jax.experimental import pallas as pl
from jax.experimental.pallas import tpu as pltpu
from jax.sharding import PartitionSpec as P

MESH = pl.DeviceIdType.MESH
HD = 128
NH = 3
ROWS = 256
WID = NH * HD
D = 3072
OWN = 192
EPS = 1e-06
INV_ROOT = 1.0 / math.sqrt(HD)
EXP2_SCALE = INV_ROOT * math.log2(math.e)
BF = jnp.bfloat16
F32 = jnp.float32
GATHER_COPIES = 32
SCATTER_COPIES = 17
QKV_FIRST, OUT_FIRST, KV_FIRST, DKV_FIRST = 320, 112, 144, 432


def dot(a, b):
    return jnp.dot(a, b, preferred_element_type=F32)


def dot_nt(a, b):
    return lax.dot_general(a, b, (((1,), (1,)), ((), ())), preferred_element_type=F32)


def at_tile(z, x, c):
    return z * 8 + x * 2 + c


class Place:
    def __init__(self):
        t = lax.axis_index("tile")
        self.me = t
        self.z, self.x, self.c = t // 8, (t // 2) % 4, t % 2
        self.xr, self.xl, self.xo = (self.x + 1) % 4, (self.x + 3) % 4, (self.x + 2) % 4
        self.right = at_tile(self.z, self.xr, self.c)
        self.left = at_tile(self.z, self.xl, self.c)
        self.across = at_tile(1 - self.z, self.x, self.c)
        self.sib = at_tile(self.z, self.x, 1 - self.c)


def split_rows(rows, first):
    def halves(start, size, up):
        half = size // 32 * 16 + (16 if up and size % 32 else 0)
        return pl.ds(start, size), (pl.ds(start, half), pl.ds(start + half, size - half))
    a, ah = halves(0, first, True)
    b, bh = halves(first, rows - first, False)
    return a, ah, b, bh


class Gather:
    def __init__(self, place, buf, first, send, recv):
        self.p, self.buf, self.send, self.recv = place, buf, send, recv
        self.a, self.ah, self.b, self.bh = split_rows(buf.shape[1], first)
        self.sent = []

    def copy(self, k, ref, dev):
        return pltpu.make_async_remote_copy(
            src_ref=ref, dst_ref=ref, send_sem=self.send.at[k], recv_sem=self.recv.at[k],
            device_id={"tile": dev}, device_id_type=MESH)

    def go(self, k, t, rows, dev):
        c = self.copy(k, self.buf.at[t, rows], dev)
        c.start()
        self.sent.append(c)

    def got(self, k, t, rows):
        self.copy(k, self.buf.at[t, rows], self.p.sib).wait_recv()

    def start(self):
        p = self.p
        self.go(0, p.me, self.a, p.across)
        self.go(1, p.me, self.b, p.right)
        self.go(2, p.me, self.b, p.left)
        self.go(3, p.me, self.a, p.right)
        self.go(4, p.me, self.a, p.left)
        self.go(5, p.me, self.b, p.across)
        c = self.copy(6, self.buf.at[p.me], p.sib)
        c.start()
        self.sent.append(c)

    def step_across(self):
        p = self.p
        self.got(0, p.across, self.a)
        self.go(7, p.across, self.a, p.right)
        self.go(8, p.across, self.a, p.left)
        self.go(9, p.across, self.a, p.sib)

    def step_sides(self):
        p = self.p
        self.got(1, p.left, self.b)
        self.go(10, p.left, self.bh[0], p.right)
        self.go(11, p.left, self.b, p.across)
        self.got(2, p.right, self.b)
        self.go(12, p.right, self.bh[1], p.left)
        self.go(13, p.right, self.b, p.across)
        self.got(3, p.left, self.a)
        self.go(14, p.left, self.ah[0], p.right)
        self.got(4, p.right, self.a)
        self.go(15, p.right, self.ah[1], p.left)
        self.go(16, p.left, self.b, p.sib)
        self.go(17, p.right, self.b, p.sib)
        self.go(18, p.left, self.a, p.sib)
        self.go(19, p.right, self.a, p.sib)
        self.got(5, p.across, self.b)
        self.go(20, p.across, self.b, p.sib)

    def step_sides_across(self):
        p = self.p
        zl, zr = at_tile(1 - p.z, p.xl, p.c), at_tile(1 - p.z, p.xr, p.c)
        self.got(7, zl, self.a)
        self.go(21, zl, self.ah[0], p.right)
        self.got(8, zr, self.a)
        self.go(22, zr, self.ah[1], p.left)
        self.go(23, zl, self.a, p.sib)
        self.go(24, zr, self.a, p.sib)

    def step_opposite(self):
        p = self.p
        zl, zr = at_tile(1 - p.z, p.xl, p.c), at_tile(1 - p.z, p.xr, p.c)
        to = at_tile(p.z, p.xo, p.c)
        self.got(10, to, self.bh[0])
        self.got(12, to, self.bh[1])
        self.go(25, to, self.b, p.across)
        self.got(14, to, self.ah[0])
        self.got(15, to, self.ah[1])
        c = self.copy(26, self.buf.at[to], p.sib)
        c.start()
        self.sent.append(c)
        self.got(11, zl, self.b)
        self.go(27, zl, self.b, p.sib)
        self.got(13, zr, self.b)
        self.go(28, zr, self.b, p.sib)

    def step_last(self):
        p = self.p
        zo = at_tile(1 - p.z, p.xo, p.c)
        self.got(21, zo, self.ah[0])
        self.got(22, zo, self.ah[1])
        self.go(29, zo, self.a, p.sib)
        self.got(25, zo, self.b)
        self.go(30, zo, self.b, p.sib)

    def sib_own(self):
        self.copy(6, self.buf.at[self.p.sib], self.p.sib).wait_recv()

    def sib_across(self):
        p = self.p
        t = at_tile(1 - p.z, p.x, 1 - p.c)
        self.got(9, t, self.a)
        self.got(20, t, self.b)

    def sib_sides(self):
        p = self.p
        tl, tr = at_tile(p.z, p.xl, 1 - p.c), at_tile(p.z, p.xr, 1 - p.c)
        self.got(16, tl, self.b)
        self.got(17, tr, self.b)
        self.got(18, tl, self.a)
        self.got(19, tr, self.a)

    def sib_sides_across(self):
        p = self.p
        zl, zr = at_tile(1 - p.z, p.xl, 1 - p.c), at_tile(1 - p.z, p.xr, 1 - p.c)
        self.got(23, zl, self.a)
        self.got(24, zr, self.a)
        self.got(27, zl, self.b)
        self.got(28, zr, self.b)

    def sib_opposite(self):
        p = self.p
        self.copy(26, self.buf.at[at_tile(p.z, p.xo, 1 - p.c)], p.sib).wait_recv()

    def sib_last(self):
        p = self.p
        zo = at_tile(1 - p.z, p.xo, 1 - p.c)
        self.got(29, zo, self.a)
        self.got(30, zo, self.b)

    def finish(self):
        for c in self.sent:
            c.wait_send()


class Scatter:
    def __init__(self, axis, ring, pair, devices, parts, first, bufs, send, recv):
        self.axis, self.ring, self.pair = axis, ring, pair
        self.right, self.left, self.across = devices
        self.parts = parts
        self.far, self.near, self.last = bufs[:3]
        self.zed, self.far_b, self.near_b = bufs[3:] if len(bufs) > 3 else (None, None, None)
        self.send, self.recv = send, recv
        self.rr, self.rl, self.ro = (ring + 1) % 4, (ring + 3) % 4, (ring + 2) % 4
        self.a, self.ah, self.b, self.bh = split_rows(parts.shape[2], first)
        self.first = first
        self.bl = [pl.ds(h.start - first, h.size) for h in self.bh]
        self.sent = []

    def copy(self, k, src, dst, dev):
        return pltpu.make_async_remote_copy(
            src_ref=src, dst_ref=dst, send_sem=self.send.at[k], recv_sem=self.recv.at[k],
            device_id={self.axis: dev}, device_id_type=MESH)

    def go(self, k, src, dst, dev):
        c = self.copy(k, src, dst, dev)
        c.start()
        self.sent.append(c)

    def got(self, k, dst):
        self.copy(k, dst, dst, self.right).wait_recv()

    def add(self, ring, pair, rows, got):
        self.parts[ring, pair, rows] = (
            self.parts[ring, pair, rows].astype(F32) + got.astype(F32)).astype(BF)

    def start_z(self, k, ring):
        self.go(k, self.parts.at[ring, 1 - self.pair, self.b], self.zed.at[ring], self.across)

    def got_z(self, k, ring):
        self.got(k, self.zed.at[ring])

    def start_far(self):
        if self.zed is not None:
            self.start_z(0, self.ro)
        for i, dev in enumerate((self.right, self.left)):
            self.go(4 + i, self.parts.at[self.ro, :, self.ah[i]], self.far.at[i, :, pl.ds(0, self.ah[i].size)], dev)

    def start_near(self):
        if self.zed is not None:
            self.start_z(1, self.rr)
            self.start_z(2, self.rl)
        self.go(6, self.parts.at[self.rr, :, self.ah[1]], self.near.at[0, :, self.ah[1]], self.right)
        self.go(7, self.parts.at[self.rl, :, self.ah[0]], self.near.at[1, :, self.ah[0]], self.left)

    def start_own(self):
        self.start_z(3, self.ring)

    def step_far_b(self):
        self.got_z(0, self.ro)
        self.add(self.ro, self.pair, self.b, self.zed[self.ro])
        for i, dev in enumerate((self.right, self.left)):
            self.go(10 + i, self.parts.at[self.ro, self.pair, self.bh[i]], self.far_b.at[i, pl.ds(0, self.bh[i].size)], dev)

    def step_near(self):
        for i, (ring, dev) in enumerate(((self.rr, self.right), (self.rl, self.left))):
            got = self.far.at[i, :, pl.ds(0, self.ah[i].size)]
            self.got(4 + i, got)
            for z in range(2):
                self.add(ring, z, self.ah[i], got[z])
            self.go(8 + i, self.parts.at[ring, :, self.ah[i]], self.near.at[i, :, self.ah[i]], dev)

    def step_near_b(self):
        for i, (ring, dev) in enumerate(((self.rr, self.right), (self.rl, self.left))):
            self.got_z(1 + i, ring)
            self.add(ring, self.pair, self.b, self.zed[ring])
            j = 1 - i
            self.go(12 + i, self.parts.at[ring, self.pair, self.bh[j]], self.near_b.at[i, self.bl[j]], dev)
        for i, (ring, dev) in enumerate(((self.rr, self.right), (self.rl, self.left))):
            got = self.far_b.at[i, pl.ds(0, self.bh[i].size)]
            self.got(10 + i, got)
            self.add(ring, self.pair, self.bh[i], got[...])
            self.go(14 + i, self.parts.at[ring, self.pair, self.bh[i]], self.near_b.at[i, self.bl[i]], dev)

    def total(self, pair):
        return (self.parts[self.ring, pair, self.a].astype(F32) + self.near[0, pair].astype(F32)
                + self.near[1, pair].astype(F32))

    def step_pair(self):
        for i in range(2):
            self.got(6 + i, self.near.at[i, :, self.ah[1 - i]])
            self.got(8 + i, self.near.at[i, :, self.ah[i]])
        other = 1 - self.pair
        self.parts[self.ring, other, self.a] = self.total(other).astype(BF)
        self.go(16, self.parts.at[self.ring, other, self.a], self.last, self.across)

    def result(self, out):
        if self.zed is not None:
            self.got_z(3, self.ring)
            for i in range(2):
                self.got(12 + i, self.near_b.at[i, self.bl[1 - i]])
                self.got(14 + i, self.near_b.at[i, self.bl[i]])
            out[self.b] = (
                (self.parts[self.ring, self.pair, self.b].astype(F32) + self.zed[self.ring].astype(F32))
                + (self.near_b[0].astype(F32) + self.near_b[1].astype(F32))).astype(out.dtype)
        self.got(16, self.last)
        out[self.a] = (self.total(self.pair) + self.last[...].astype(F32)).astype(out.dtype)

    def finish(self):
        for c in self.sent:
            c.wait_send()


def kernel(tok_hbm, cot_hbm, w_hbm, wo_hbm, slab, ext,
           out_ref, gtok_ref, gqkv_ref, gout_ref,
           w, wo, kv, tok, cot, tok_t, tok_sib, cot_t, cot_sib, wexp, mask,
           proj, q, qt, g, gt, num, den, delta, dq, att, gp, dkv_sum,
           dkv_out, dkv_parts, dkv_far, dkv_near, dkv_last, dkv_zed, dkv_far_b, dkv_near_b,
           gq_parts, gq_far, gq_near, gq_last, gq_zed, gq_far_b, gq_near_b,
           go_parts, go_far, go_near, go_last, go_zed, go_far_b, go_near_b,
           hd_parts, ho_far, ho_near, ho_last, ht_far, ht_near, ht_last,
           load_sem, gat_send, gat_recv, sca_send, sca_recv, sib_send, sib_recv, dkv_send, dkv_recv):
    p = Place()
    hd = lax.axis_index("head")
    hy, hz = hd // 2, hd % 2
    head_devices = (((hy + 1) % 4) * 2 + hz, ((hy + 3) % 4) * 2 + hz, hy * 2 + 1 - hz)
    lane_devices = (p.right, p.left, p.across)

    loads = [pltpu.make_async_copy(a, b, load_sem.at[i]) for i, (a, b) in enumerate((
        (w_hbm, w.at[p.me]), (wo_hbm, wo.at[p.me]), (tok_hbm, tok), (cot_hbm, cot)))]
    for c in loads:
        c.start()

    barrier = pltpu.get_barrier_semaphore()
    for dev in (p.right, p.left, p.across, p.sib):
        pl.semaphore_signal(barrier, inc=1, device_id={"tile": dev}, device_id_type=MESH)
    for dev in head_devices:
        pl.semaphore_signal(barrier, inc=1, device_id={"head": dev}, device_id_type=MESH)
    pl.semaphore_wait(barrier, 7)

    sent = []

    def to_sibling(k, src, dst):
        c = pltpu.make_async_remote_copy(
            src_ref=src, dst_ref=dst, send_sem=sib_send.at[k], recv_sem=sib_recv.at[k],
            device_id={"tile": p.sib}, device_id_type=MESH)
        c.start()
        sent.append(c)
        return c

    gather_w = Gather(p, w, QKV_FIRST, gat_send.at[0], gat_recv.at[0])
    gather_o = Gather(p, wo, OUT_FIRST, gat_send.at[1], gat_recv.at[1])
    gather_kv = Gather(p, kv, KV_FIRST, gat_send.at[2], gat_recv.at[2])
    scatter = lambda i, parts, first, *bufs: Scatter(
        "tile", p.x, p.z, lane_devices, parts, first, bufs, sca_send.at[i], sca_recv.at[i])
    head_scatter = lambda i, parts, *bufs: Scatter(
        "head", hy, hz, head_devices, parts, ROWS, bufs, sca_send.at[i], sca_recv.at[i])
    sum_dkv = scatter(0, dkv_parts, DKV_FIRST, dkv_far, dkv_near, dkv_last, dkv_zed, dkv_far_b, dkv_near_b)
    sum_gq = scatter(1, gq_parts, QKV_FIRST, gq_far, gq_near, gq_last, gq_zed, gq_far_b, gq_near_b)
    sum_go = scatter(2, go_parts, OUT_FIRST, go_far, go_near, go_last, go_zed, go_far_b, go_near_b)
    sum_out = head_scatter(3, hd_parts, ho_far, ho_near, ho_last)
    sum_tok = head_scatter(4, hd_parts, ht_far, ht_near, ht_last)

    loads[0].wait()
    gather_w.start()

    height = lax.rem(slab[p.me], 4)
    near_height = lax.rem(slab[p.sib], 4)
    far_height = lax.rem(slab[at_tile(p.z, p.xr, 1 - p.c)], 4)
    key_width = lax.broadcasted_iota(jnp.int32, (64, ROWS), 1) // 64
    for qw in range(4):
        reach_h = ext[0, height * 4 + qw]
        reach_w = ext[1, height * 4 + qw]
        near_w = jnp.where(jnp.abs(key_width - qw) <= reach_w, 1.0, 0.0)
        for m, other in enumerate((height, near_height, far_height)):
            gap = jnp.full((64, ROWS), jnp.abs(height - other), jnp.int32)
            mask[m, qw * 64:(qw + 1) * 64] = jnp.where(gap <= reach_h, near_w, 0.0)

    loads[2].wait()
    loads[3].wait()

    def turn(src, dst):
        def body(j, carry):
            cols = pl.ds(pl.multiple_of(j * 384, 384), 384)
            dst[j] = src[:, cols].T.reshape(2, OWN, ROWS)
            return carry
        lax.fori_loop(0, 8, body, 0)

    turn(tok, tok_t)
    tok_swap = to_sibling(0, tok_t.at[:, 1 - p.c], tok_sib)
    turn(cot, cot_t)
    cot_swap = to_sibling(1, cot_t.at[:, 1 - p.c], cot_sib)

    def project(z, x, first=False):
        j = z * 4 + x
        t = tok[:, pl.ds(pl.multiple_of(j * 384, 384), 384)]
        for i in range(3):
            chunk = w[pl.ds(2 * j, 2), i * OWN:(i + 1) * OWN, :].reshape(2 * OWN, WID)
            if first:
                proj[i] = dot(t, chunk)
            else:
                proj[i] += dot(t, chunk)

    gather_w.step_across()
    gather_w.sib_own()
    project(p.z, p.x, True)
    gather_w.step_sides()
    loads[1].wait()
    gather_o.start()
    gather_w.sib_across()
    project(1 - p.z, p.x)
    gather_w.step_sides_across()
    gather_w.sib_sides()
    project(p.z, p.xl)
    project(p.z, p.xr)
    gather_w.step_opposite()
    gather_o.step_across()
    gather_w.sib_sides_across()
    project(1 - p.z, p.xl)
    project(1 - p.z, p.xr)
    gather_w.sib_opposite()
    project(p.z, p.xo)
    gather_w.step_last()
    gather_o.step_sides()
    gather_w.sib_last()
    project(1 - p.z, p.xo)

    def scale_of(raw):
        return lax.rsqrt(jnp.mean(raw * raw, axis=-1, keepdims=True) + EPS)

    for h in range(NH):
        hs = slice(h * HD, (h + 1) * HD)
        raw = proj[1, :, hs]
        kv[p.me, :, hs] = (raw * scale_of(raw)).astype(BF)
    kv[p.me, :, WID:] = proj[2].astype(BF)
    gather_kv.start()
    for h in range(NH):
        hs = slice(h * HD, (h + 1) * HD)
        raw = proj[0, :, hs]
        unit = (raw * scale_of(raw)).astype(BF)
        q[:, hs] = unit
        qt[h] = unit.T

    def forward(t, m, i, first=False):
        for h in range(NH):
            hs = slice(h * HD, (h + 1) * HD)
            vs = slice(WID + h * HD, WID + (h + 1) * HD)
            scores = dot_nt(q[:, hs], kv[t, :, hs])
            we = jnp.exp2(scores * EXP2_SCALE) * mask[m]
            wexp[i, h] = we
            part = we[:, :HD] + we[:, HD:]
            val = dot(we.astype(BF), kv[t, :, vs])
            if first:
                den[h] = part
                num[:, hs] = val
            else:
                den[h] += part
                num[:, hs] += val

    def loop2(fn):
        lax.fori_loop(0, 2, lambda i, carry: (fn(i), carry)[1], 0)

    gather_o.step_sides_across()
    forward(p.me, 0, 0, True)
    gather_kv.step_across()
    gather_kv.sib_own()
    forward(p.sib, 1, 2)
    gather_o.step_opposite()
    gather_kv.step_sides()
    forward(p.across, 0, 1)
    gather_o.step_last()
    gather_kv.sib_across()
    forward(at_tile(1 - p.z, p.x, 1 - p.c), 1, 3)
    gather_kv.step_sides_across()
    gather_o.sib_own()
    gather_o.sib_across()
    gather_o.sib_sides()
    gather_o.sib_sides_across()
    gather_o.sib_opposite()
    gather_o.sib_last()

    def grad_att(j, acc):
        cols = pl.ds(pl.multiple_of(j * 384, 384), 384)
        return acc + dot(cot[:, cols], wo[pl.ds(2 * j, 2)].reshape(2 * OWN, WID))

    g[...] = lax.fori_loop(0, 8, grad_att, jnp.zeros((ROWS, WID), F32)).astype(BF)
    for h in range(NH):
        gt[h] = g[:, h * HD:(h + 1) * HD].T
    def side(zz, i):
        forward(at_tile(zz, p.xl, 1 - p.c), 2, 4 + 2 * i)
        forward(at_tile(zz, p.xr, 1 - p.c), 2, 5 + 2 * i)

    gather_kv.sib_sides()
    side(p.z, 0)
    gather_kv.step_opposite()
    forward(at_tile(p.z, p.xo, p.c), 0, 8)
    gather_kv.sib_sides_across()
    side(1 - p.z, 1)
    gather_kv.step_last()
    gather_kv.sib_opposite()
    forward(at_tile(p.z, p.xo, 1 - p.c), 1, 10)
    forward(at_tile(1 - p.z, p.xo, p.c), 0, 9)
    gather_kv.sib_last()
    forward(at_tile(1 - p.z, p.xo, 1 - p.c), 1, 11)

    for h in range(NH):
        hs = slice(h * HD, (h + 1) * HD)
        inverse = 1.0 / jnp.sum(den[h], axis=-1, keepdims=True)
        context = num[:, hs] * inverse
        att[0, :, hs] = context.astype(BF)
        row = jnp.sum(g[:, hs].astype(F32) * context, axis=-1, keepdims=True)
        delta[h] = jnp.broadcast_to(row, (ROWS, HD))
        den[h] = jnp.broadcast_to(inverse, (ROWS, HD))
    att_swap = to_sibling(2, att.at[0], att.at[1])

    def backward(t, i, dst, first=False, adding=False):
        for h in range(NH):
            hs = slice(h * HD, (h + 1) * HD)
            vs = slice(WID + h * HD, WID + (h + 1) * HD)
            grad = dot_nt(g[:, hs], kv[t, :, vs])
            inverse, row = den[h], delta[h]
            probs, ds = [], []
            for part in range(2):
                cs = slice(part * HD, (part + 1) * HD)
                pr = wexp[i, h, :, cs] * inverse
                ds.append((pr * (grad[:, cs] - row)).astype(BF))
                probs.append(pr.astype(BF))
            probs = jnp.concatenate(probs, axis=1)
            ds = jnp.concatenate(ds, axis=1)
            term = dot(ds, kv[t, :, hs])
            if first:
                dq[:, hs] = term
            else:
                dq[:, hs] += term
            dk = dot(qt[h], ds) * INV_ROOT
            dv = dot(gt[h], probs)
            if adding:
                dk = dk + dst[hs].astype(F32)
                dv = dv + dst[vs].astype(F32)
            dst[hs] = dk.astype(BF)
            dst[vs] = dv.astype(BF)

    def swap_copy(x, z, k):
        return pltpu.make_async_remote_copy(
            src_ref=dkv_out.at[x, z], dst_ref=dkv_parts.at[x, z], send_sem=dkv_send.at[k],
            recv_sem=dkv_recv.at[k], device_id={"tile": p.sib}, device_id_type=MESH)

    def swap(x, z, k):
        c = swap_copy(x, z, k)
        c.start()
        sent.append(c)

    def out_part(j, carry):
        hd_parts[j // 2, j % 2] = dot_nt(att[0], wo[pl.ds(2 * j, 2)].reshape(2 * OWN, WID)).astype(BF)
        return carry

    def opposite_sib(i):
        zz = (p.z + i) % 2
        backward(at_tile(zz, p.xo, 1 - p.c), 10 + i, dkv_out.at[p.xo, zz])

    def out_grad(j, carry):
        go_parts[j % 4, j // 4] = (dot(cot_t[j, p.c], att[0]) + dot(cot_sib[j], att[1])).astype(BF)
        return carry

    cot_swap.wait_recv()
    att_swap.wait_recv()
    lax.fori_loop(0, 8, out_grad, 0)
    sum_go.start_far()
    sum_go.start_near()
    sum_go.start_own()

    dq[...] = jnp.zeros_like(dq)
    loop2(opposite_sib)
    swap(p.xo, p.z, 0)
    swap(p.xo, 1 - p.z, 1)
    lax.fori_loop(0, 8, out_part, 0)
    sum_out.start_far()
    sum_out.start_near()
    for i, zz in enumerate((p.z, 1 - p.z)):
        swap_copy(p.xo, zz, i).wait_recv()

    def opposite_own(i):
        zz = (p.z + i) % 2
        backward(at_tile(zz, p.xo, p.c), 8 + i, dkv_parts.at[p.xo, zz], adding=True)

    loop2(opposite_own)
    sum_dkv.start_far()
    sum_go.step_far_b()
    sum_go.step_near()

    def sides_sib(i):
        zz = (p.z + i) % 2
        backward(at_tile(zz, p.xl, 1 - p.c), 4 + 2 * i, dkv_out.at[p.xl, zz])
        backward(at_tile(zz, p.xr, 1 - p.c), 5 + 2 * i, dkv_out.at[p.xr, zz])

    loop2(sides_sib)
    for i, zz in enumerate((p.z, 1 - p.z)):
        swap(p.xl, zz, 2 + i)
        swap(p.xr, zz, 4 + i)
    sum_dkv.step_far_b()
    sum_go.step_near_b()
    for i, zz in enumerate((p.z, 1 - p.z)):
        swap_copy(p.xl, zz, 2 + i).wait_recv()
        swap_copy(p.xr, zz, 4 + i).wait_recv()
    sum_dkv.start_near()
    sum_out.step_near()

    def own_sib(i):
        zz = (p.z + i) % 2
        backward(at_tile(zz, p.x, 1 - p.c), 2 + i, dkv_out.at[p.x, zz])

    loop2(own_sib)
    for i, zz in enumerate((p.z, 1 - p.z)):
        swap(p.x, zz, 6 + i)
    sum_dkv.step_near()
    sum_dkv.step_near_b()
    for i, zz in enumerate((p.z, 1 - p.z)):
        swap_copy(p.x, zz, 6 + i).wait_recv()

    def own_own(i):
        zz = (p.z + i) % 2
        backward(at_tile(zz, p.x, p.c), i, dkv_parts.at[p.x, zz], adding=True)

    loop2(own_own)
    sum_dkv.start_own()

    def unit_back(grad, raw):
        scale = scale_of(raw)
        unit = raw * scale
        return scale * (grad - unit * jnp.mean(grad * unit, axis=-1, keepdims=True))

    for h in range(NH):
        hs = slice(h * HD, (h + 1) * HD)
        gp[0, 0, :, hs] = unit_back(dq[:, hs] * INV_ROOT, proj[0, :, hs]).astype(BF)
    sum_go.step_pair()
    sum_dkv.step_pair()
    sum_out.step_pair()
    sum_dkv.result(dkv_sum)
    for h in range(NH):
        hs = slice(h * HD, (h + 1) * HD)
        vs = slice(WID + h * HD, WID + (h + 1) * HD)
        gp[0, 1, :, hs] = unit_back(dkv_sum[hs].T, proj[1, :, hs]).astype(BF)
        gp[0, 2, :, hs] = dkv_sum[vs].T.astype(BF)
    gp_swap = to_sibling(3, gp.at[0], gp.at[1])

    tok_swap.wait_recv()
    gp_swap.wait_recv()

    def qkv_grad(j):
        for i in range(3):
            gq_parts[j % 4, j // 4, i * OWN:(i + 1) * OWN] = (
                dot(tok_t[j, p.c], gp[0, i]) + dot(tok_sib[j], gp[1, i])).astype(BF)

    loop2(lambda i: qkv_grad(i * 4 + p.xo))
    sum_gq.start_far()
    loop2(lambda i: qkv_grad(i * 4 + p.xr))
    loop2(lambda i: qkv_grad(i * 4 + p.xl))
    sum_gq.start_near()
    loop2(lambda i: qkv_grad(i * 4 + p.x))
    sum_gq.start_own()
    sum_out.result(out_ref)
    sum_out.finish()

    def tok_part(j, carry):
        acc = dot_nt(gp[0, 0], w[pl.ds(2 * j, 2), 0:OWN, :].reshape(2 * OWN, WID))
        for i in range(1, 3):
            acc += dot_nt(gp[0, i], w[pl.ds(2 * j, 2), i * OWN:(i + 1) * OWN, :].reshape(2 * OWN, WID))
        hd_parts[j // 2, j % 2] = acc.astype(BF)
        return carry

    lax.fori_loop(0, 8, tok_part, 0)
    sum_tok.start_far()
    sum_tok.start_near()
    sum_gq.step_far_b()
    sum_gq.step_near()
    sum_gq.step_near_b()
    sum_tok.step_near()
    sum_go.result(gout_ref)
    sum_gq.step_pair()
    sum_tok.step_pair()
    sum_gq.result(gqkv_ref)
    sum_tok.result(gtok_ref)

    for s in (gather_w, gather_o, gather_kv, sum_dkv, sum_gq, sum_go, sum_tok):
        s.finish()
    for c in sent:
        c.wait_send()


def lane_bufs(rows, first, cols):
    _, ah, _, bh = split_rows(rows, first)
    second = rows - first
    bufs = [(2, 2, ah[0].size, cols), (2, 2, first, cols), (first, cols)]
    if second:
        bufs += [(4, second, cols), (2, bh[1].size, cols), (2, second, cols)]
    return [pltpu.VMEM(b, BF) for b in bufs]


def deliver(*refs):
    for i in range(4):
        refs[4 + i][...] = refs[i][...]


def local(tokens, cotangent, qkv_weight, out_weight, slab_of_device, extents):
    w = jnp.transpose(qkv_weight, (1, 0, 2)).reshape(3 * OWN, WID)
    vm = lambda *shape, dtype=BF: pltpu.VMEM(shape, dtype)
    dma = lambda *shape: pltpu.SemaphoreType.DMA(shape)
    scratch = [
        vm(16, 3 * OWN, WID), vm(16, OWN, WID), vm(16, ROWS, 2 * WID), vm(ROWS, D), vm(ROWS, D),
        vm(8, 2, OWN, ROWS), vm(8, OWN, ROWS), vm(8, 2, OWN, ROWS), vm(8, OWN, ROWS),
        vm(12, NH, ROWS, ROWS, dtype=F32), vm(3, ROWS, ROWS, dtype=F32),
        vm(3, ROWS, WID, dtype=F32), vm(ROWS, WID), vm(NH, HD, ROWS), vm(ROWS, WID), vm(NH, HD, ROWS),
        vm(ROWS, WID, dtype=F32), vm(NH, ROWS, HD, dtype=F32), vm(NH, ROWS, HD, dtype=F32),
        vm(ROWS, WID, dtype=F32), vm(2, ROWS, WID), vm(2, 3, ROWS, WID), vm(2 * WID, ROWS, dtype=F32),
        vm(4, 2, 2 * WID, ROWS), vm(4, 2, 2 * WID, ROWS), *lane_bufs(2 * WID, DKV_FIRST, ROWS),
        vm(4, 2, 3 * OWN, WID), *lane_bufs(3 * OWN, QKV_FIRST, WID),
        vm(4, 2, OWN, WID), *lane_bufs(OWN, OUT_FIRST, WID),
        vm(4, 2, ROWS, WID), *lane_bufs(ROWS, ROWS, WID), *lane_bufs(ROWS, ROWS, WID),
        dma(4), dma(3, GATHER_COPIES), dma(3, GATHER_COPIES), dma(5, SCATTER_COPIES), dma(5, SCATTER_COPIES),
        dma(4), dma(4), dma(8), dma(8),
    ]
    any_spec = pl.BlockSpec(memory_space=pl.ANY)
    smem = pl.BlockSpec(memory_space=pltpu.SMEM)
    vmem = pl.BlockSpec(memory_space=pltpu.VMEM)
    shapes = (
        jax.ShapeDtypeStruct((ROWS, WID), BF), jax.ShapeDtypeStruct((ROWS, WID), BF),
        jax.ShapeDtypeStruct((3 * OWN, WID), F32), jax.ShapeDtypeStruct((OWN, WID), F32))
    results = pl.pallas_call(
        kernel,
        out_shape=shapes,
        in_specs=[any_spec] * 4 + [smem] * 2,
        out_specs=(vmem,) * 4,
        scratch_shapes=scratch,
        compiler_params=pltpu.CompilerParams(
            collective_id=0, has_side_effects=True, vmem_limit_bytes=64 * 1024 * 1024),
        cost_estimate=pl.CostEstimate(flops=20_000_000_000, bytes_accessed=10_000_000, transcendentals=2_400_000),
        name="sublayer",
    )(tokens, cotangent, w, out_weight, slab_of_device, extents.T)
    output, grad_tokens, grad_qkv, grad_out = pl.pallas_call(
        deliver, out_shape=shapes, in_specs=[vmem] * 4, out_specs=(vmem,) * 4, name="deliver")(*results)
    grad_qkv = jnp.transpose(grad_qkv.reshape(3, OWN, WID), (1, 0, 2))
    return output, grad_tokens, grad_qkv, grad_out


def solution(mesh):
    return jax.shard_map(
        local, mesh=mesh,
        in_specs=(P("tile", None), P("tile", None), P("tile", None, "head"), P("tile", "head"), P(None), P(None, None)),
        out_specs=(P("tile", "head"), P("tile", "head"), P("tile", None, "head"), P("tile", "head")),
        check_vma=False)
```

```python
import math

import jax
import jax.numpy as jnp
from jax import lax
from jax.experimental import pallas as pl
from jax.experimental.pallas import tpu as pltpu
from jax.sharding import PartitionSpec as P

MESH = pl.DeviceIdType.MESH
HD = 128
NH = 3
ROWS = 256
WID = NH * HD
D = 3072
OWN = 192
EPS = 1e-06
INV_ROOT = 1.0 / math.sqrt(HD)
EXP2_SCALE = INV_ROOT * math.log2(math.e)
BF = jnp.bfloat16
F32 = jnp.float32
GATHER_COPIES = 32
SCATTER_COPIES = 23
SUM_FIRST = 128
QKV_FIRST, OUT_FIRST, KV_FIRST, DKV_FIRST, KVW_FIRST = 320, 112, 144, 496, 256


def dot(a, b):
    return jnp.dot(a, b, preferred_element_type=F32)


def dot_nt(a, b):
    return lax.dot_general(a, b, (((1,), (1,)), ((), ())), preferred_element_type=F32)


def at_tile(z, x, c):
    return z * 8 + x * 2 + c


class Place:
    def __init__(self):
        t = lax.axis_index("tile")
        self.me = t
        self.z, self.x, self.c = t // 8, (t // 2) % 4, t % 2
        self.xr, self.xl, self.xo = (self.x + 1) % 4, (self.x + 3) % 4, (self.x + 2) % 4
        self.right = at_tile(self.z, self.xr, self.c)
        self.left = at_tile(self.z, self.xl, self.c)
        self.across = at_tile(1 - self.z, self.x, self.c)
        self.sib = at_tile(self.z, self.x, 1 - self.c)


def split_rows(rows, first):
    def halves(start, size, up):
        half = size // 32 * 16 + (16 if up and size % 32 else 0)
        return pl.ds(start, size), (pl.ds(start, half), pl.ds(start + half, size - half))
    a, ah = halves(0, first, True)
    b, bh = halves(first, rows - first, False)
    return a, ah, b, bh


class Gather:
    def __init__(self, place, buf, first, send, recv):
        self.p, self.buf, self.send, self.recv = place, buf, send, recv
        self.a, self.ah, self.b, self.bh = split_rows(buf.shape[1], first)
        self.sent = []

    def copy(self, k, ref, dev):
        return pltpu.make_async_remote_copy(
            src_ref=ref, dst_ref=ref, send_sem=self.send.at[k], recv_sem=self.recv.at[k],
            device_id={"tile": dev}, device_id_type=MESH)

    def go(self, k, t, rows, dev):
        c = self.copy(k, self.buf.at[t, rows], dev)
        c.start()
        self.sent.append(c)

    def got(self, k, t, rows):
        self.copy(k, self.buf.at[t, rows], self.p.sib).wait_recv()

    def start(self):
        p = self.p
        self.go(0, p.me, self.a, p.across)
        self.go(1, p.me, self.b, p.right)
        self.go(2, p.me, self.b, p.left)
        c = self.copy(6, self.buf.at[p.me], p.sib)
        c.start()
        self.sent.append(c)

    def start_rest(self, in_turn):
        p = self.p
        if in_turn:
            for c in self.sent[1:3]:
                c.wait_send()
        self.go(3, p.me, self.a, p.right)
        self.go(4, p.me, self.a, p.left)
        if in_turn:
            self.sent[0].wait_send()
            del self.sent[:3]
        self.go(5, p.me, self.b, p.across)

    def step_across(self):
        p = self.p
        self.got(0, p.across, self.a)
        self.go(7, p.across, self.a, p.right)
        self.go(8, p.across, self.a, p.left)
        self.go(9, p.across, self.a, p.sib)

    def step_sides(self):
        p = self.p
        self.got(1, p.left, self.b)
        self.go(10, p.left, self.bh[0], p.right)
        self.go(11, p.left, self.b, p.across)
        self.got(2, p.right, self.b)
        self.go(12, p.right, self.bh[1], p.left)
        self.go(13, p.right, self.b, p.across)
        self.got(3, p.left, self.a)
        self.go(14, p.left, self.ah[0], p.right)
        self.got(4, p.right, self.a)
        self.go(15, p.right, self.ah[1], p.left)
        self.go(16, p.left, self.b, p.sib)
        self.go(17, p.right, self.b, p.sib)
        self.go(18, p.left, self.a, p.sib)
        self.go(19, p.right, self.a, p.sib)

    def step_sides_across(self):
        p = self.p
        zl, zr = at_tile(1 - p.z, p.xl, p.c), at_tile(1 - p.z, p.xr, p.c)
        to = at_tile(p.z, p.xo, p.c)
        self.got(10, to, self.bh[0])
        self.got(12, to, self.bh[1])
        self.go(25, to, self.b, p.across)
        self.got(7, zl, self.a)
        self.go(21, zl, self.ah[0], p.right)
        self.got(8, zr, self.a)
        self.go(22, zr, self.ah[1], p.left)
        self.go(23, zl, self.a, p.sib)
        self.go(24, zr, self.a, p.sib)
        self.got(5, p.across, self.b)
        self.go(20, p.across, self.b, p.sib)

    def step_opposite(self):
        p = self.p
        zl, zr = at_tile(1 - p.z, p.xl, p.c), at_tile(1 - p.z, p.xr, p.c)
        to = at_tile(p.z, p.xo, p.c)
        self.got(14, to, self.ah[0])
        self.got(15, to, self.ah[1])
        c = self.copy(26, self.buf.at[to], p.sib)
        c.start()
        self.sent.append(c)
        self.got(11, zl, self.b)
        self.go(27, zl, self.b, p.sib)
        self.got(13, zr, self.b)
        self.go(28, zr, self.b, p.sib)

    def step_last(self):
        p = self.p
        zo = at_tile(1 - p.z, p.xo, p.c)
        self.got(21, zo, self.ah[0])
        self.got(22, zo, self.ah[1])
        self.go(29, zo, self.a, p.sib)
        self.got(25, zo, self.b)
        self.go(30, zo, self.b, p.sib)

    def sib_own(self):
        self.copy(6, self.buf.at[self.p.sib], self.p.sib).wait_recv()

    def sib_across(self):
        p = self.p
        t = at_tile(1 - p.z, p.x, 1 - p.c)
        self.got(9, t, self.a)
        self.got(20, t, self.b)

    def sib_sides(self):
        p = self.p
        tl, tr = at_tile(p.z, p.xl, 1 - p.c), at_tile(p.z, p.xr, 1 - p.c)
        self.got(16, tl, self.b)
        self.got(17, tr, self.b)
        self.got(18, tl, self.a)
        self.got(19, tr, self.a)

    def sib_sides_across(self):
        p = self.p
        zl, zr = at_tile(1 - p.z, p.xl, 1 - p.c), at_tile(1 - p.z, p.xr, 1 - p.c)
        self.got(23, zl, self.a)
        self.got(24, zr, self.a)
        self.got(27, zl, self.b)
        self.got(28, zr, self.b)

    def sib_opposite(self):
        p = self.p
        self.copy(26, self.buf.at[at_tile(p.z, p.xo, 1 - p.c)], p.sib).wait_recv()

    def sib_last(self):
        p = self.p
        zo = at_tile(1 - p.z, p.xo, 1 - p.c)
        self.got(29, zo, self.a)
        self.got(30, zo, self.b)

    def finish(self):
        for c in self.sent:
            c.wait_send()


class Scatter:
    def __init__(self, axis, ring, pair, devices, parts, first, bufs, send, recv):
        self.axis, self.ring, self.pair = axis, ring, pair
        self.right, self.left, self.across = devices
        self.parts = parts
        self.far, self.near, self.last = bufs[:3]
        self.zed, self.far_b, self.near_b = bufs[3:] if len(bufs) > 3 else (None, None, None)
        self.send, self.recv = send, recv
        self.rr, self.rl, self.ro = (ring + 1) % 4, (ring + 3) % 4, (ring + 2) % 4
        self.a, self.ah, self.b, self.bh = split_rows(parts.shape[2], first)
        self.first = first
        self.bl = [pl.ds(h.start - first, h.size) for h in self.bh]
        self.sent = []

    def copy(self, k, src, dst, dev):
        return pltpu.make_async_remote_copy(
            src_ref=src, dst_ref=dst, send_sem=self.send.at[k], recv_sem=self.recv.at[k],
            device_id={self.axis: dev}, device_id_type=MESH)

    def go(self, k, src, dst, dev):
        c = self.copy(k, src, dst, dev)
        c.start()
        self.sent.append(c)

    def got(self, k, dst):
        self.copy(k, dst, dst, self.right).wait_recv()

    def add(self, ring, pair, rows, got):
        self.parts[ring, pair, rows] = (
            self.parts[ring, pair, rows].astype(F32) + got.astype(F32)).astype(BF)


    def pairs(self):
        return (0, 1 - self.pair), (1, self.pair)

    def start_z(self, k, ring):
        if self.zed is not None:
            self.go(k, self.parts.at[ring, 1 - self.pair, self.b], self.zed.at[ring], self.across)

    def got_z(self, k, ring):
        self.got(k, self.zed.at[ring])

    def far_at(self, i, n):
        return self.far.at[i, n, pl.ds(0, self.ah[i].size)]

    def start_far(self, n, over=True):
        z = self.pairs()[n][1]
        for i, dev in enumerate((self.right, self.left)):
            self.go(4 + 2 * n + i, self.parts.at[self.ro, z, self.ah[i]], self.far_at(i, n), dev)
        if n == 0 and over:
            self.start_z(0, self.ro)

    def start_near(self, n, over=True):
        z = self.pairs()[n][1]
        for i, (ring, dev) in enumerate(((self.rr, self.right), (self.rl, self.left))):
            rows = self.ah[1 - i]
            self.go(8 + 2 * n + i, self.parts.at[ring, z, rows], self.near.at[i, n, rows], dev)
            if n == 0 and over:
                self.start_z(1 + i, ring)

    def start_own(self):
        self.start_z(3, self.ring)

    def start_over(self):
        for k, ring in enumerate((self.ro, self.rr, self.rl, self.ring)):
            self.start_z(k, ring)

    def step_far_b(self):
        self.got_z(0, self.ro)
        self.add(self.ro, self.pair, self.b, self.zed[self.ro])
        for i, dev in enumerate((self.right, self.left)):
            self.go(16 + i, self.parts.at[self.ro, self.pair, self.bh[i]], self.far_b.at[i, pl.ds(0, self.bh[i].size)], dev)

    def step_near(self, n):
        z = self.pairs()[n][1]
        for i, (ring, dev) in enumerate(((self.rr, self.right), (self.rl, self.left))):
            rows, got = self.ah[i], self.far_at(i, n)
            self.got(4 + 2 * n + i, got)
            self.add(ring, z, rows, got[...])
            self.go(12 + 2 * n + i, self.parts.at[ring, z, rows], self.near.at[i, n, rows], dev)

    def step_near_b(self):
        for i, (ring, dev) in enumerate(((self.rr, self.right), (self.rl, self.left))):
            self.got_z(1 + i, ring)
            self.add(ring, self.pair, self.b, self.zed[ring])
            j = 1 - i
            self.go(18 + i, self.parts.at[ring, self.pair, self.bh[j]], self.near_b.at[i, self.bl[j]], dev)
        for i, (ring, dev) in enumerate(((self.rr, self.right), (self.rl, self.left))):
            got = self.far_b.at[i, pl.ds(0, self.bh[i].size)]
            self.got(16 + i, got)
            self.add(ring, self.pair, self.bh[i], got[...])
            self.go(20 + i, self.parts.at[ring, self.pair, self.bh[i]], self.near_b.at[i, self.bl[i]], dev)

    def total(self, n):
        for i in range(2):
            self.got(8 + 2 * n + i, self.near.at[i, n, self.ah[1 - i]])
            self.got(12 + 2 * n + i, self.near.at[i, n, self.ah[i]])
        z = self.pairs()[n][1]
        return (self.parts[self.ring, z, self.a].astype(F32) + self.near[0, n].astype(F32)
                + self.near[1, n].astype(F32))

    def step_pair(self):
        other = 1 - self.pair
        self.parts[self.ring, other, self.a] = self.total(0).astype(BF)
        self.go(22, self.parts.at[self.ring, other, self.a], self.last, self.across)

    def result_b(self, out):
        self.got_z(3, self.ring)
        for i in range(2):
            self.got(18 + i, self.near_b.at[i, self.bl[1 - i]])
            self.got(20 + i, self.near_b.at[i, self.bl[i]])
        out[self.b] = (
            (self.parts[self.ring, self.pair, self.b].astype(F32) + self.zed[self.ring].astype(F32))
            + (self.near_b[0].astype(F32) + self.near_b[1].astype(F32))).astype(out.dtype)

    def result_a(self, out):
        own = self.total(1)
        self.got(22, self.last)
        out[self.a] = (own + self.last[...].astype(F32)).astype(out.dtype)

    def finish(self):
        for c in self.sent:
            c.wait_send()


def kernel(tok_hbm, cot_hbm, w_hbm, wo_hbm, slab, ext,
           out_ref, gtok_ref, gqkv_ref, gout_ref,
           w, wo, kv, tok, cot, tok_t, tok_sib, cot_t, cot_sib, wexp, mask,
           proj, q, qt, g, gt, num, den, delta, dq, att, gp, dkv_sum,
           dkv_out, dkv_parts, dkv_far, dkv_near, dkv_last, dkv_zed, dkv_far_b, dkv_near_b,
           gq_parts, gq_far, gq_near, gq_last, gq_zed, gq_far_b, gq_near_b,
           gk_parts, gk_far, gk_near, gk_last, gk_zed, gk_far_b, gk_near_b,
           go_parts, go_far, go_near, go_last, go_zed, go_far_b, go_near_b,
           ho_parts, ho_far, ho_near, ho_last, ht_parts, ht_far, ht_near, ht_last,
           load_sem, gat_send, gat_recv, sca_send, sca_recv, sib_send, sib_recv, dkv_send, dkv_recv):
    p = Place()
    hd = lax.axis_index("head")
    hy, hz = hd // 2, hd % 2
    head_devices = (((hy + 1) % 4) * 2 + hz, ((hy + 3) % 4) * 2 + hz, hy * 2 + 1 - hz)
    lane_devices = (p.right, p.left, p.across)

    loads = [pltpu.make_async_copy(a, b, load_sem.at[i]) for i, (a, b) in enumerate((
        (w_hbm, w.at[p.me]), (wo_hbm, wo.at[p.me]), (tok_hbm, tok), (cot_hbm, cot)))]
    for c in loads:
        c.start()

    barrier = pltpu.get_barrier_semaphore()
    for dev in (p.right, p.left, p.across, p.sib):
        pl.semaphore_signal(barrier, inc=1, device_id={"tile": dev}, device_id_type=MESH)
    for dev in head_devices:
        pl.semaphore_signal(barrier, inc=1, device_id={"head": dev}, device_id_type=MESH)
    pl.semaphore_wait(barrier, 7)

    sent = []

    def to_sibling(k, src, dst):
        c = pltpu.make_async_remote_copy(
            src_ref=src, dst_ref=dst, send_sem=sib_send.at[k], recv_sem=sib_recv.at[k],
            device_id={"tile": p.sib}, device_id_type=MESH)
        c.start()
        sent.append(c)
        return c

    gather_w = Gather(p, w, QKV_FIRST, gat_send.at[0], gat_recv.at[0])
    gather_o = Gather(p, wo, OUT_FIRST, gat_send.at[1], gat_recv.at[1])
    gather_kv = Gather(p, kv, KV_FIRST, gat_send.at[2], gat_recv.at[2])
    scatter = lambda i, parts, first, *bufs: Scatter(
        "tile", p.x, p.z, lane_devices, parts, first, bufs, sca_send.at[i], sca_recv.at[i])
    head_scatter = lambda i, parts, *bufs: Scatter(
        "head", hy, hz, head_devices, parts, ROWS, bufs, sca_send.at[i], sca_recv.at[i])
    sum_dkv = scatter(0, dkv_parts, DKV_FIRST, dkv_far, dkv_near, dkv_last, dkv_zed, dkv_far_b, dkv_near_b)
    sum_gk = scatter(5, gk_parts, KVW_FIRST, gk_far, gk_near, gk_last, gk_zed, gk_far_b, gk_near_b)
    sum_gq = scatter(1, gq_parts, SUM_FIRST, gq_far, gq_near, gq_last, gq_zed, gq_far_b, gq_near_b)
    sum_go = scatter(2, go_parts, SUM_FIRST, go_far, go_near, go_last, go_zed, go_far_b, go_near_b)
    sum_out = head_scatter(3, ho_parts, ho_far, ho_near, ho_last)
    sum_tok = head_scatter(4, ht_parts, ht_far, ht_near, ht_last)

    loads[0].wait()
    gather_w.start()

    height = lax.rem(slab[p.me], 4)
    near_height = lax.rem(slab[p.sib], 4)
    far_height = lax.rem(slab[at_tile(p.z, p.xr, 1 - p.c)], 4)
    key_width = lax.broadcasted_iota(jnp.int32, (64, ROWS), 1) // 64
    for qw in range(4):
        reach_h = ext[0, height * 4 + qw]
        reach_w = ext[1, height * 4 + qw]
        near_w = jnp.where(jnp.abs(key_width - qw) <= reach_w, 1.0, 0.0)
        for m, other in enumerate((height, near_height, far_height)):
            gap = jnp.full((64, ROWS), jnp.abs(height - other), jnp.int32)
            mask[m, qw * 64:(qw + 1) * 64] = jnp.where(gap <= reach_h, near_w, 0.0)

    loads[2].wait()
    loads[3].wait()

    def turn(src, dst):
        def body(j, carry):
            cols = pl.ds(pl.multiple_of(j * 384, 384), 384)
            dst[j] = src[:, cols].T.reshape(2, OWN, ROWS)
            return carry
        lax.fori_loop(0, 8, body, 0)

    turn(tok, tok_t)
    tok_swap = to_sibling(0, tok_t.at[:, 1 - p.c], tok_sib)
    turn(cot, cot_t)
    cot_swap = to_sibling(1, cot_t.at[:, 1 - p.c], cot_sib)

    def project(z, x, first=False):
        j = z * 4 + x
        t = tok[:, pl.ds(pl.multiple_of(j * 384, 384), 384)]
        for i in range(3):
            chunk = w[pl.ds(2 * j, 2), i * OWN:(i + 1) * OWN, :].reshape(2 * OWN, WID)
            if first:
                proj[i] = dot(t, chunk)
            else:
                proj[i] += dot(t, chunk)

    gather_w.start_rest(True)
    gather_w.step_across()
    gather_w.sib_own()
    project(p.z, p.x, True)
    gather_w.step_sides()
    loads[1].wait()
    gather_o.start()
    gather_o.start_rest(False)
    gather_w.sib_sides()
    project(p.z, p.xl)
    project(p.z, p.xr)
    gather_w.step_sides_across()
    gather_o.step_across()
    gather_w.sib_across()
    project(1 - p.z, p.x)
    gather_w.step_opposite()
    gather_o.step_sides()
    gather_w.sib_sides_across()
    project(1 - p.z, p.xl)
    project(1 - p.z, p.xr)
    gather_w.sib_opposite()
    project(p.z, p.xo)
    gather_w.step_last()
    gather_o.step_sides_across()
    gather_w.sib_last()
    project(1 - p.z, p.xo)

    def scale_of(raw):
        return lax.rsqrt(jnp.mean(raw * raw, axis=-1, keepdims=True) + EPS)

    for h in range(NH):
        hs = slice(h * HD, (h + 1) * HD)
        raw = proj[1, :, hs]
        kv[p.me, :, hs] = (raw * scale_of(raw)).astype(BF)
    kv[p.me, :, WID:] = proj[2].astype(BF)
    gather_kv.start()
    for h in range(NH):
        hs = slice(h * HD, (h + 1) * HD)
        raw = proj[0, :, hs]
        unit = (raw * scale_of(raw)).astype(BF)
        q[:, hs] = unit
        qt[h] = unit.T

    def forward(t, m, i, first=False):
        for h in range(NH):
            hs = slice(h * HD, (h + 1) * HD)
            vs = slice(WID + h * HD, WID + (h + 1) * HD)
            scores = dot_nt(q[:, hs], kv[t, :, hs])
            we = jnp.exp2(scores * EXP2_SCALE) * mask[m]
            wexp[i, h] = we
            part = we[:, :HD] + we[:, HD:]
            val = dot(we.astype(BF), kv[t, :, vs])
            if first:
                den[h] = part
                num[:, hs] = val
            else:
                den[h] += part
                num[:, hs] += val

    def loop2(fn):
        lax.fori_loop(0, 2, lambda i, carry: (fn(i), carry)[1], 0)

    def grad_att(j, acc):
        cols = pl.ds(pl.multiple_of(j * 384, 384), 384)
        return acc + dot(cot[:, cols], wo[pl.ds(2 * j, 2)].reshape(2 * OWN, WID))

    def side(zz, i):
        forward(at_tile(zz, p.xl, 1 - p.c), 2, 4 + 2 * i)
        forward(at_tile(zz, p.xr, 1 - p.c), 2, 5 + 2 * i)

    forward(p.me, 0, 0, True)
    gather_kv.start_rest(True)
    gather_kv.step_across()
    gather_kv.sib_own()
    gather_o.step_opposite()
    forward(p.sib, 1, 2)
    gather_kv.step_sides()
    gather_kv.step_sides_across()
    forward(p.across, 0, 1)
    gather_kv.sib_sides()
    side(p.z, 0)
    gather_o.step_last()
    gather_kv.sib_across()
    forward(at_tile(1 - p.z, p.x, 1 - p.c), 1, 3)
    gather_kv.step_opposite()
    forward(at_tile(p.z, p.xo, p.c), 0, 8)
    gather_kv.sib_sides_across()
    side(1 - p.z, 1)
    gather_o.sib_own()
    gather_o.sib_across()
    gather_o.sib_sides()
    gather_o.sib_sides_across()
    gather_o.sib_opposite()
    gather_o.sib_last()
    g[...] = lax.fori_loop(0, 8, grad_att, jnp.zeros((ROWS, WID), F32)).astype(BF)
    for h in range(NH):
        gt[h] = g[:, h * HD:(h + 1) * HD].T
    gather_kv.step_last()
    gather_kv.sib_opposite()
    forward(at_tile(p.z, p.xo, 1 - p.c), 1, 10)
    forward(at_tile(1 - p.z, p.xo, p.c), 0, 9)
    gather_kv.sib_last()
    forward(at_tile(1 - p.z, p.xo, 1 - p.c), 1, 11)

    for h in range(NH):
        hs = slice(h * HD, (h + 1) * HD)
        inverse = 1.0 / jnp.sum(den[h], axis=-1, keepdims=True)
        context = num[:, hs] * inverse
        att[0, :, hs] = context.astype(BF)
        row = jnp.sum(g[:, hs].astype(F32) * context, axis=-1, keepdims=True)
        delta[h] = jnp.broadcast_to(row, (ROWS, HD))
        den[h] = jnp.broadcast_to(inverse, (ROWS, HD))
    att_swap = to_sibling(2, att.at[0], att.at[1])

    def backward(t, i, dst, first=False, adding=False):
        for h in range(NH):
            hs = slice(h * HD, (h + 1) * HD)
            vs = slice(WID + h * HD, WID + (h + 1) * HD)
            grad = dot_nt(g[:, hs], kv[t, :, vs])
            inverse, row = den[h], delta[h]
            probs, ds = [], []
            for part in range(2):
                cs = slice(part * HD, (part + 1) * HD)
                pr = wexp[i, h, :, cs] * inverse
                ds.append((pr * (grad[:, cs] - row)).astype(BF))
                probs.append(pr.astype(BF))
            probs = jnp.concatenate(probs, axis=1)
            ds = jnp.concatenate(ds, axis=1)
            term = dot(ds, kv[t, :, hs])
            if first:
                dq[:, hs] = term
            else:
                dq[:, hs] += term
            dk = dot(qt[h], ds) * INV_ROOT
            dv = dot(gt[h], probs)
            if adding:
                dk = dk + dst[hs].astype(F32)
                dv = dv + dst[vs].astype(F32)
            dst[hs] = dk.astype(BF)
            dst[vs] = dv.astype(BF)

    def swap_copy(x, z, k):
        return pltpu.make_async_remote_copy(
            src_ref=dkv_out.at[x, z], dst_ref=dkv_parts.at[x, z], send_sem=dkv_send.at[k],
            recv_sem=dkv_recv.at[k], device_id={"tile": p.sib}, device_id_type=MESH)

    def swap(x, z, k):
        c = swap_copy(x, z, k)
        c.start()
        sent.append(c)

    def out_part(ring):
        def one(i):
            o = wo[pl.ds(4 * ring + 2 * i, 2)].reshape(2 * OWN, WID)
            ho_parts[ring, i] = dot_nt(att[0], o).astype(BF)
        loop2(one)

    def tok_part(ring):
        def one(i):
            j = 2 * ring + i
            acc = dot_nt(gp[0, 0], w[pl.ds(2 * j, 2), 0:OWN, :].reshape(2 * OWN, WID))
            for n in range(1, 3):
                acc += dot_nt(gp[0, n], w[pl.ds(2 * j, 2), n * OWN:(n + 1) * OWN, :].reshape(2 * OWN, WID))
            ht_parts[ring, i] = acc.astype(BF)
        loop2(one)

    def out_grad(ring):
        def one(i):
            j = 4 * i + ring
            go_parts[ring, i] = (dot(cot_t[j, p.c], att[0]) + dot(cot_sib[j], att[1])).astype(BF)
        loop2(one)

    def qkv_grad(parts, j, which):
        for n, i in enumerate(which):
            parts[j % 4, j // 4, n * OWN:(n + 1) * OWN] = (
                dot(tok_t[j, p.c], gp[0, i]) + dot(tok_sib[j], gp[1, i])).astype(BF)

    def kv_grad(ring):
        loop2(lambda i: qkv_grad(gk_parts, i * 4 + ring, (1, 2)))

    def opposite_sib(i):
        zz = (p.z + i) % 2
        backward(at_tile(zz, p.xo, 1 - p.c), 10 + i, dkv_out.at[p.xo, zz])

    def opposite_own(i):
        zz = (p.z + 1 + i) % 2
        backward(at_tile(zz, p.xo, p.c), 9 - i, dkv_parts.at[p.xo, zz], adding=True)

    def sides_sib(i):
        zz = (p.z + 1 + i) % 2
        backward(at_tile(zz, p.xl, 1 - p.c), 6 - 2 * i, dkv_out.at[p.xl, zz])
        backward(at_tile(zz, p.xr, 1 - p.c), 7 - 2 * i, dkv_out.at[p.xr, zz])

    def own_sib(i):
        zz = (p.z + i) % 2
        backward(at_tile(zz, p.x, 1 - p.c), 2 + i, dkv_out.at[p.x, zz])

    def own_own(i):
        zz = (p.z + i) % 2
        backward(at_tile(zz, p.x, p.c), i, dkv_parts.at[p.x, zz], adding=True)

    def unit_back(grad, raw):
        scale = scale_of(raw)
        unit = raw * scale
        return scale * (grad - unit * jnp.mean(grad * unit, axis=-1, keepdims=True))

    dq[...] = jnp.zeros_like(dq)
    loop2(opposite_sib)
    swap(p.xo, 1 - p.z, 0)
    swap(p.xo, p.z, 1)
    cot_swap.wait_recv()
    att_swap.wait_recv()
    out_grad(p.xo)
    sum_go.start_far(0, False)
    sum_go.start_far(1, False)
    out_grad(p.xr)
    out_grad(p.xl)
    sum_go.start_near(0, False)
    sum_go.start_near(1, False)
    swap_copy(p.xo, 1 - p.z, 0).wait_recv()
    swap_copy(p.xo, p.z, 1).wait_recv()
    loop2(opposite_own)
    sum_dkv.start_far(0)
    sum_dkv.start_far(1)
    sides_sib(0)
    swap(p.xl, 1 - p.z, 2)
    swap(p.xr, 1 - p.z, 3)
    sides_sib(1)
    swap(p.xl, p.z, 4)
    swap(p.xr, p.z, 5)
    out_part(sum_out.ro)
    sum_out.start_far(0)
    sum_out.start_far(1)
    swap_copy(p.xl, 1 - p.z, 2).wait_recv()
    swap_copy(p.xr, 1 - p.z, 3).wait_recv()
    sum_dkv.start_near(0)
    out_part(sum_out.rr)
    out_part(sum_out.rl)
    sum_out.start_near(0)
    sum_out.start_near(1)
    swap_copy(p.xl, p.z, 4).wait_recv()
    swap_copy(p.xr, p.z, 5).wait_recv()
    sum_dkv.start_near(1)
    loop2(own_sib)
    swap(p.x, p.z, 6)
    swap(p.x, 1 - p.z, 7)
    sum_dkv.step_near(0)
    sum_dkv.step_far_b()
    sum_dkv.step_near(1)
    sum_go.step_near(0)
    sum_go.step_near(1)
    swap_copy(p.x, p.z, 6).wait_recv()
    swap_copy(p.x, 1 - p.z, 7).wait_recv()
    loop2(own_own)
    sum_dkv.start_own()
    out_grad(p.x)
    sum_go.start_over()
    for h in range(NH):
        hs = slice(h * HD, (h + 1) * HD)
        gp[0, 0, :, hs] = unit_back(dq[:, hs] * INV_ROOT, proj[0, :, hs]).astype(BF)
    gq_swap = to_sibling(3, gp.at[0, 0], gp.at[1, 0])
    out_part(sum_out.ring)
    sum_out.step_near(0)
    sum_out.step_near(1)
    sum_dkv.step_near_b()

    tok_swap.wait_recv()
    gq_swap.wait_recv()
    lax.fori_loop(0, 8, lambda j, carry: (qkv_grad(gq_parts, j, (0,)), carry)[1], 0)
    sum_gq.start_far(0, False)
    sum_gq.start_far(1, False)
    sum_gq.start_near(0, False)
    sum_gq.start_near(1, False)
    sum_dkv.step_pair()
    sum_dkv.result_b(dkv_sum)
    sum_out.step_pair()
    sum_dkv.result_a(dkv_sum)
    sum_gq.start_over()
    for h in range(NH):
        hs = slice(h * HD, (h + 1) * HD)
        vs = slice(WID + h * HD, WID + (h + 1) * HD)
        gp[0, 1, :, hs] = unit_back(dkv_sum[hs].T, proj[1, :, hs]).astype(BF)
        gp[0, 2, :, hs] = dkv_sum[vs].T.astype(BF)
    gk_swap = to_sibling(4, gp.at[0, pl.ds(1, 2)], gp.at[1, pl.ds(1, 2)])

    sum_go.step_far_b()
    tok_part(sum_tok.ro)
    sum_tok.start_far(0)
    sum_tok.start_far(1)
    gk_swap.wait_recv()
    kv_grad(p.xo)
    sum_gk.start_far(0)
    sum_gk.start_far(1)
    sum_go.step_pair()
    sum_gq.step_near(0)
    sum_gq.step_near(1)
    sum_go.step_near_b()
    tok_part(sum_tok.rr)
    tok_part(sum_tok.rl)
    sum_tok.start_near(0)
    sum_tok.start_near(1)
    kv_grad(p.xr)
    kv_grad(p.xl)
    sum_gk.start_near(0)
    sum_gk.start_near(1)
    sum_gq.step_far_b()
    tok_part(sum_tok.ring)
    sum_tok.step_near(0)
    sum_tok.step_near(1)
    kv_grad(p.x)
    sum_gk.start_own()
    sum_gk.step_near(0)
    sum_gq.step_near_b()
    sum_gk.step_far_b()
    sum_gk.step_near(1)
    sum_out.result_a(out_ref)
    sum_go.result_b(gout_ref)
    sum_go.result_a(gout_ref)
    sum_tok.step_pair()
    sum_gq.step_pair()
    sum_gk.step_near_b()
    sum_gk.step_pair()
    sum_gq.result_b(gqkv_ref.at[pl.ds(0, OWN)])
    sum_gq.result_a(gqkv_ref.at[pl.ds(0, OWN)])
    sum_tok.result_a(gtok_ref)
    sum_gk.result_b(gqkv_ref.at[pl.ds(OWN, 2 * OWN)])
    sum_gk.result_a(gqkv_ref.at[pl.ds(OWN, 2 * OWN)])

    for s in (gather_w, gather_o, gather_kv, sum_dkv, sum_gq, sum_gk, sum_go, sum_out, sum_tok):
        s.finish()
    for c in sent:
        c.wait_send()


def lane_bufs(rows, first, cols):
    _, ah, _, bh = split_rows(rows, first)
    second = rows - first
    bufs = [(2, 2, ah[0].size, cols), (2, 2, first, cols), (first, cols)]
    if second:
        bufs += [(4, second, cols), (2, bh[1].size, cols), (2, second, cols)]
    return [pltpu.VMEM(b, BF) for b in bufs]


def deliver(*refs):
    for i in range(4):
        refs[4 + i][...] = refs[i][...]


def local(tokens, cotangent, qkv_weight, out_weight, slab_of_device, extents):
    w = jnp.transpose(qkv_weight, (1, 0, 2)).reshape(3 * OWN, WID)
    vm = lambda *shape, dtype=BF: pltpu.VMEM(shape, dtype)
    dma = lambda *shape: pltpu.SemaphoreType.DMA(shape)
    scratch = [
        vm(16, 3 * OWN, WID), vm(16, OWN, WID), vm(16, ROWS, 2 * WID), vm(ROWS, D), vm(ROWS, D),
        vm(8, 2, OWN, ROWS), vm(8, OWN, ROWS), vm(8, 2, OWN, ROWS), vm(8, OWN, ROWS),
        vm(12, NH, ROWS, ROWS, dtype=F32), vm(3, ROWS, ROWS, dtype=F32),
        vm(3, ROWS, WID, dtype=F32), vm(ROWS, WID), vm(NH, HD, ROWS), vm(ROWS, WID), vm(NH, HD, ROWS),
        vm(ROWS, WID, dtype=F32), vm(NH, ROWS, HD, dtype=F32), vm(NH, ROWS, HD, dtype=F32),
        vm(ROWS, WID, dtype=F32), vm(2, ROWS, WID), vm(2, 3, ROWS, WID), vm(2 * WID, ROWS, dtype=F32),
        vm(4, 2, 2 * WID, ROWS), vm(4, 2, 2 * WID, ROWS), *lane_bufs(2 * WID, DKV_FIRST, ROWS),
        vm(4, 2, OWN, WID), *lane_bufs(OWN, SUM_FIRST, WID),
        vm(4, 2, 2 * OWN, WID), *lane_bufs(2 * OWN, KVW_FIRST, WID),
        vm(4, 2, OWN, WID), *lane_bufs(OWN, SUM_FIRST, WID),
        vm(4, 2, ROWS, WID), *lane_bufs(ROWS, ROWS, WID), vm(4, 2, ROWS, WID), *lane_bufs(ROWS, ROWS, WID),
        dma(4), dma(3, GATHER_COPIES), dma(3, GATHER_COPIES), dma(6, SCATTER_COPIES), dma(6, SCATTER_COPIES),
        dma(5), dma(5), dma(8), dma(8),
    ]
    any_spec = pl.BlockSpec(memory_space=pl.ANY)
    smem = pl.BlockSpec(memory_space=pltpu.SMEM)
    vmem = pl.BlockSpec(memory_space=pltpu.VMEM)
    shapes = (
        jax.ShapeDtypeStruct((ROWS, WID), BF), jax.ShapeDtypeStruct((ROWS, WID), BF),
        jax.ShapeDtypeStruct((3 * OWN, WID), F32), jax.ShapeDtypeStruct((OWN, WID), F32))
    results = pl.pallas_call(
        kernel,
        out_shape=shapes,
        in_specs=[any_spec] * 4 + [smem] * 2,
        out_specs=(vmem,) * 4,
        scratch_shapes=scratch,
        compiler_params=pltpu.CompilerParams(
            collective_id=0, has_side_effects=True, vmem_limit_bytes=64 * 1024 * 1024),
        cost_estimate=pl.CostEstimate(flops=20_000_000_000, bytes_accessed=10_000_000, transcendentals=2_400_000),
        name="sublayer",
    )(tokens, cotangent, w, out_weight, slab_of_device, extents.T)
    output, grad_tokens, grad_qkv, grad_out = pl.pallas_call(
        deliver, out_shape=shapes, in_specs=[vmem] * 4, out_specs=(vmem,) * 4, name="deliver")(*results)
    grad_qkv = jnp.transpose(grad_qkv.reshape(3, OWN, WID), (1, 0, 2))
    return output, grad_tokens, grad_qkv, grad_out


def solution(mesh):
    return jax.shard_map(
        local, mesh=mesh,
        in_specs=(P("tile", None), P("tile", None), P("tile", None, "head"), P("tile", "head"), P(None), P(None, None)),
        out_specs=(P("tile", "head"), P("tile", "head"), P("tile", None, "head"), P("tile", "head")),
        check_vma=False)
```

```python
import math

import jax
import jax.numpy as jnp
from jax import lax
from jax.experimental import pallas as pl
from jax.experimental.pallas import tpu as pltpu
from jax.sharding import PartitionSpec as P

MESH = pl.DeviceIdType.MESH
HD = 128
NH = 3
ROWS = 256
WID = NH * HD
D = 3072
OWN = 192
EPS = 1e-06
INV_ROOT = 1.0 / math.sqrt(HD)
EXP2_SCALE = INV_ROOT * math.log2(math.e)
BF = jnp.bfloat16
F32 = jnp.float32
GATHER_TWO, GATHER_ONE = range(31), (0, 3, 4, 6, 7, 8, 9, 14, 15, 18, 19, 21, 22, 23, 24, 26, 29)
SUM_TWO, SUM_ONE = range(23), (*range(4, 16), 22)
W_AT, O_AT, KB_AT, KA_AT, DB_AT, GO_AT, DA_AT, OUT_AT, TOK_AT, SEMS = 0, 31, 62, 93, 110, 133, 156, 169, 182, 195
SUM_FIRST = 144
QKV_FIRST, OUT_FIRST, KV_FIRST, DKV_FIRST, KVW_FIRST = 320, 112, 64, 64, 304


def dot(a, b):
    return jnp.dot(a, b, preferred_element_type=F32)


def dot_nt(a, b):
    return lax.dot_general(a, b, (((1,), (1,)), ((), ())), preferred_element_type=F32)


def at_tile(z, x, c):
    return z * 8 + x * 2 + c


class Place:
    def __init__(self):
        t = lax.axis_index("tile")
        self.me = t
        self.z, self.x, self.c = t // 8, (t // 2) % 4, t % 2
        self.xr, self.xl, self.xo = (self.x + 1) % 4, (self.x + 3) % 4, (self.x + 2) % 4
        self.right = at_tile(self.z, self.xr, self.c)
        self.left = at_tile(self.z, self.xl, self.c)
        self.across = at_tile(1 - self.z, self.x, self.c)
        self.sib = at_tile(self.z, self.x, 1 - self.c)


def split_rows(rows, first):
    def halves(start, size, up):
        half = size // 32 * 16 + (16 if up and size % 32 else 0)
        return pl.ds(start, size), (pl.ds(start, half), pl.ds(start + half, size - half))
    a, ah = halves(0, first, True)
    b, bh = halves(first, rows - first, False)
    return a, ah, b, bh


class Sems:
    def __init__(self, send, recv, base, keys):
        self.send, self.recv, self.base, self.keys = send, recv, base, tuple(keys)

    def __call__(self, k):
        i = self.base + self.keys.index(k)
        return dict(send_sem=self.send.at[i], recv_sem=self.recv.at[i])


class Gather:
    def __init__(self, place, buf, first, sems, for_across=None):
        self.p, self.buf, self.sems = place, buf, sems
        self.two, self.for_across = first < buf.shape[1], for_across
        self.a, self.ah, self.b, self.bh = split_rows(buf.shape[1], first)
        self.sent = []

    def copy(self, k, ref, dev):
        return pltpu.make_async_remote_copy(
            src_ref=ref, dst_ref=ref, **self.sems(k), device_id={"tile": dev}, device_id_type=MESH)

    def go(self, k, t, rows, dev):
        c = self.copy(k, self.buf.at[t, rows], dev)
        c.start()
        self.sent.append(c)

    def got(self, k, t, rows):
        self.copy(k, self.buf.at[t, rows], self.p.sib).wait_recv()

    def start(self):
        p = self.p
        if self.two:
            self.go(0, p.me, self.a, p.across)
            self.go(1, p.me, self.b, p.right)
            self.go(2, p.me, self.b, p.left)
        else:
            c = pltpu.make_async_remote_copy(
                src_ref=self.for_across, dst_ref=self.buf.at[p.me], **self.sems(0),
                device_id={"tile": p.across}, device_id_type=MESH)
            c.start()
            self.sent.append(c)
            self.go(3, p.me, self.a, p.right)
            self.go(4, p.me, self.a, p.left)
        c = self.copy(6, self.buf.at[p.me], p.sib)
        c.start()
        self.sent.append(c)

    def start_rest(self, in_turn):
        p = self.p
        if in_turn:
            for c in self.sent[1:3]:
                c.wait_send()
        self.go(3, p.me, self.a, p.right)
        self.go(4, p.me, self.a, p.left)
        if in_turn:
            self.sent[0].wait_send()
            del self.sent[:3]
        self.go(5, p.me, self.b, p.across)

    def step_across(self):
        p = self.p
        self.got(0, p.across, self.a)
        self.go(7, p.across, self.a, p.right)
        self.go(8, p.across, self.a, p.left)
        self.go(9, p.across, self.a, p.sib)

    def step_sides(self):
        p = self.p
        if self.two:
            self.got(1, p.left, self.b)
            self.go(10, p.left, self.bh[0], p.right)
            self.go(11, p.left, self.b, p.across)
            self.got(2, p.right, self.b)
            self.go(12, p.right, self.bh[1], p.left)
            self.go(13, p.right, self.b, p.across)
        self.got(3, p.left, self.a)
        self.go(14, p.left, self.ah[0], p.right)
        self.got(4, p.right, self.a)
        self.go(15, p.right, self.ah[1], p.left)
        if self.two:
            self.go(16, p.left, self.b, p.sib)
            self.go(17, p.right, self.b, p.sib)
        self.go(18, p.left, self.a, p.sib)
        self.go(19, p.right, self.a, p.sib)

    def step_sides_across(self):
        p = self.p
        zl, zr = at_tile(1 - p.z, p.xl, p.c), at_tile(1 - p.z, p.xr, p.c)
        to = at_tile(p.z, p.xo, p.c)
        if self.two:
            self.got(10, to, self.bh[0])
            self.got(12, to, self.bh[1])
            self.go(25, to, self.b, p.across)
        self.got(7, zl, self.a)
        self.go(21, zl, self.ah[0], p.right)
        self.got(8, zr, self.a)
        self.go(22, zr, self.ah[1], p.left)
        self.go(23, zl, self.a, p.sib)
        self.go(24, zr, self.a, p.sib)
        if self.two:
            self.got(5, p.across, self.b)
            self.go(20, p.across, self.b, p.sib)

    def step_opposite(self):
        p = self.p
        zl, zr = at_tile(1 - p.z, p.xl, p.c), at_tile(1 - p.z, p.xr, p.c)
        to = at_tile(p.z, p.xo, p.c)
        self.got(14, to, self.ah[0])
        self.got(15, to, self.ah[1])
        c = self.copy(26, self.buf.at[to], p.sib)
        c.start()
        self.sent.append(c)
        if self.two:
            self.got(11, zl, self.b)
            self.go(27, zl, self.b, p.sib)
            self.got(13, zr, self.b)
            self.go(28, zr, self.b, p.sib)

    def step_last(self):
        p = self.p
        zo = at_tile(1 - p.z, p.xo, p.c)
        self.got(21, zo, self.ah[0])
        self.got(22, zo, self.ah[1])
        self.go(29, zo, self.a, p.sib)
        if self.two:
            self.got(25, zo, self.b)
            self.go(30, zo, self.b, p.sib)

    def sib_own(self):
        self.copy(6, self.buf.at[self.p.sib], self.p.sib).wait_recv()

    def sib_across(self):
        p = self.p
        t = at_tile(1 - p.z, p.x, 1 - p.c)
        self.got(9, t, self.a)
        if self.two:
            self.got(20, t, self.b)

    def sib_sides(self):
        p = self.p
        tl, tr = at_tile(p.z, p.xl, 1 - p.c), at_tile(p.z, p.xr, 1 - p.c)
        if self.two:
            self.got(16, tl, self.b)
            self.got(17, tr, self.b)
        self.got(18, tl, self.a)
        self.got(19, tr, self.a)

    def sib_sides_across(self):
        p = self.p
        zl, zr = at_tile(1 - p.z, p.xl, 1 - p.c), at_tile(1 - p.z, p.xr, 1 - p.c)
        self.got(23, zl, self.a)
        self.got(24, zr, self.a)
        if self.two:
            self.got(27, zl, self.b)
            self.got(28, zr, self.b)

    def sib_opposite(self):
        p = self.p
        self.copy(26, self.buf.at[at_tile(p.z, p.xo, 1 - p.c)], p.sib).wait_recv()

    def sib_last(self):
        p = self.p
        zo = at_tile(1 - p.z, p.xo, 1 - p.c)
        self.got(29, zo, self.a)
        if self.two:
            self.got(30, zo, self.b)

    def finish(self):
        for c in self.sent:
            c.wait_send()


class Scatter:
    def __init__(self, axis, ring, pair, devices, parts, first, bufs, sems):
        self.axis, self.ring, self.pair = axis, ring, pair
        self.right, self.left, self.across = devices
        self.parts = parts
        self.far, self.near, self.last = bufs[:3]
        self.zed, self.far_b, self.near_b = bufs[3:] if len(bufs) > 3 else (None, None, None)
        self.sems = sems
        self.rr, self.rl, self.ro = (ring + 1) % 4, (ring + 3) % 4, (ring + 2) % 4
        self.a, self.ah, self.b, self.bh = split_rows(parts.shape[2], first)
        self.first = first
        self.bl = [pl.ds(h.start - first, h.size) for h in self.bh]
        self.sent = []

    def copy(self, k, src, dst, dev):
        return pltpu.make_async_remote_copy(
            src_ref=src, dst_ref=dst, **self.sems(k), device_id={self.axis: dev}, device_id_type=MESH)

    def go(self, k, src, dst, dev):
        c = self.copy(k, src, dst, dev)
        c.start()
        self.sent.append(c)

    def got(self, k, dst):
        self.copy(k, dst, dst, self.right).wait_recv()

    def add(self, ring, pair, rows, got):
        self.parts[ring, pair, rows] = (
            self.parts[ring, pair, rows].astype(F32) + got.astype(F32)).astype(BF)


    def pairs(self):
        return (0, 1 - self.pair), (1, self.pair)

    def start_z(self, k, ring):
        if self.zed is not None:
            self.go(k, self.parts.at[ring, 1 - self.pair, self.b], self.zed.at[ring], self.across)

    def got_z(self, k, ring):
        self.got(k, self.zed.at[ring])

    def far_at(self, i, n):
        return self.far.at[i, n, pl.ds(0, self.ah[i].size)]

    def start_far(self, n, over=True):
        z = self.pairs()[n][1]
        for i, dev in enumerate((self.right, self.left)):
            self.go(4 + 2 * n + i, self.parts.at[self.ro, z, self.ah[i]], self.far_at(i, n), dev)
        if n == 0 and over:
            self.start_z(0, self.ro)

    def start_near(self, n, over=True):
        z = self.pairs()[n][1]
        for i, (ring, dev) in enumerate(((self.rr, self.right), (self.rl, self.left))):
            rows = self.ah[1 - i]
            self.go(8 + 2 * n + i, self.parts.at[ring, z, rows], self.near.at[i, n, rows], dev)
            if n == 0 and over:
                self.start_z(1 + i, ring)

    def start_own(self):
        self.start_z(3, self.ring)

    def start_over(self):
        for k, ring in enumerate((self.ro, self.rr, self.rl, self.ring)):
            self.start_z(k, ring)

    def step_far_b(self):
        self.got_z(0, self.ro)
        self.add(self.ro, self.pair, self.b, self.zed[self.ro])
        for i, dev in enumerate((self.right, self.left)):
            self.go(16 + i, self.parts.at[self.ro, self.pair, self.bh[i]], self.far_b.at[i, pl.ds(0, self.bh[i].size)], dev)

    def step_near(self, n):
        z = self.pairs()[n][1]
        for i, (ring, dev) in enumerate(((self.rr, self.right), (self.rl, self.left))):
            rows, got = self.ah[i], self.far_at(i, n)
            self.got(4 + 2 * n + i, got)
            self.add(ring, z, rows, got[...])
            self.go(12 + 2 * n + i, self.parts.at[ring, z, rows], self.near.at[i, n, rows], dev)

    def step_near_b(self):
        for i, (ring, dev) in enumerate(((self.rr, self.right), (self.rl, self.left))):
            self.got_z(1 + i, ring)
            self.add(ring, self.pair, self.b, self.zed[ring])
            j = 1 - i
            self.go(18 + i, self.parts.at[ring, self.pair, self.bh[j]], self.near_b.at[i, self.bl[j]], dev)
        for i, (ring, dev) in enumerate(((self.rr, self.right), (self.rl, self.left))):
            got = self.far_b.at[i, pl.ds(0, self.bh[i].size)]
            self.got(16 + i, got)
            self.add(ring, self.pair, self.bh[i], got[...])
            self.go(20 + i, self.parts.at[ring, self.pair, self.bh[i]], self.near_b.at[i, self.bl[i]], dev)

    def total(self, n):
        for i in range(2):
            self.got(8 + 2 * n + i, self.near.at[i, n, self.ah[1 - i]])
            self.got(12 + 2 * n + i, self.near.at[i, n, self.ah[i]])
        z = self.pairs()[n][1]
        return (self.parts[self.ring, z, self.a].astype(F32) + self.near[0, n].astype(F32)
                + self.near[1, n].astype(F32))

    def step_pair(self):
        other = 1 - self.pair
        self.parts[self.ring, other, self.a] = self.total(0).astype(BF)
        self.go(22, self.parts.at[self.ring, other, self.a], self.last, self.across)

    def result_b(self, out):
        self.got_z(3, self.ring)
        for i in range(2):
            self.got(18 + i, self.near_b.at[i, self.bl[1 - i]])
            self.got(20 + i, self.near_b.at[i, self.bl[i]])
        out[self.b] = (
            (self.parts[self.ring, self.pair, self.b].astype(F32) + self.zed[self.ring].astype(F32))
            + (self.near_b[0].astype(F32) + self.near_b[1].astype(F32))).astype(out.dtype)

    def result_own(self, out):
        out[...] = self.total(1)

    def result_last(self, out):
        self.got(22, self.last)
        out[...] = self.last[...].astype(F32)

    def result_a(self, out):
        own = self.total(1)
        self.got(22, self.last)
        out[self.a] = (own + self.last[...].astype(F32)).astype(out.dtype)

    def finish(self):
        for c in self.sent:
            c.wait_send()


def kernel(tok_hbm, cot_hbm, w_hbm, wo_hbm, slab, ext,
           out_ref, gtok_ref, gqkv_ref, gout_ref,
           w, wo, kva, kvb, kv_out, tok, cot, tok_t, tok_sib, cot_t, cot_sib, wexp, mask,
           proj, q, qt, g_all, g, gt, num, den, delta, dq, att, gp, dkv_sum, pair_out, pair_in,
           d_out, d_parts, da_far, da_near, da_last, db_far, db_near, db_last, db_zed, db_far_b, db_near_b,
           gq_parts, gq_far, gq_near, gq_last, gq_zed, gq_far_b, gq_near_b,
           gk_parts, gk_far, gk_near, gk_last, gk_zed, gk_far_b, gk_near_b,
           go_parts, go_far, go_near, go_last, go_zed, go_far_b, go_near_b,
           ho_parts, ho_far, ho_near, ho_last, ht_parts, ht_far, ht_near, ht_last,
           load_sem, lane_send, lane_recv, sib_send, sib_recv, dkv_send, dkv_recv, pair_send, pair_recv):
    p = Place()
    hd = lax.axis_index("head")
    hy, hz = hd // 2, hd % 2
    head_devices = (((hy + 1) % 4) * 2 + hz, ((hy + 3) % 4) * 2 + hz, hy * 2 + 1 - hz)
    lane_devices = (p.right, p.left, p.across)

    loads = [pltpu.make_async_copy(a, b, load_sem.at[i]) for i, (a, b) in enumerate((
        (w_hbm, w.at[p.me]), (wo_hbm, wo.at[p.me]), (tok_hbm, tok), (cot_hbm, cot)))]
    for c in loads:
        c.start()

    barrier = pltpu.get_barrier_semaphore()
    for dev in (p.right, p.left, p.across, p.sib):
        pl.semaphore_signal(barrier, inc=1, device_id={"tile": dev}, device_id_type=MESH)
    for dev in head_devices:
        pl.semaphore_signal(barrier, inc=1, device_id={"head": dev}, device_id_type=MESH)
    pl.semaphore_wait(barrier, 7)

    sent = []

    def to_sibling(k, src, dst):
        c = pltpu.make_async_remote_copy(
            src_ref=src, dst_ref=dst, send_sem=sib_send.at[k], recv_sem=sib_recv.at[k],
            device_id={"tile": p.sib}, device_id_type=MESH)
        c.start()
        sent.append(c)
        return c

    def sems(base, keys):
        return Sems(lane_send, lane_recv, base, keys)

    gather_w = Gather(p, w, QKV_FIRST, sems(W_AT, GATHER_TWO))
    gather_o = Gather(p, wo, OUT_FIRST, sems(O_AT, GATHER_TWO))
    head_a, head_x = 2 * p.z, 2 * (1 - p.z)
    row_0 = p.z == 0

    def of_a(get):
        return jnp.where(row_0, get(slice(0, HD)), get(slice(2 * HD, 3 * HD)))

    def of_x(get):
        return jnp.where(row_0, get(slice(2 * HD, 3 * HD)), get(slice(0, HD)))

    def of_b(get):
        return get(slice(HD, 2 * HD))

    def wide(ref, *index):
        return jnp.concatenate([ref[(*index, h)] for h in range(NH)], axis=1)

    def to_across(k, dst):
        c = pltpu.make_async_remote_copy(
            src_ref=pair_out.at[k], dst_ref=dst, send_sem=pair_send.at[k], recv_sem=pair_recv.at[k],
            device_id={"tile": p.across}, device_id_type=MESH)
        c.start()
        sent.append(c)
        return c

    gather_ka = Gather(p, kva, ROWS, sems(KA_AT, GATHER_ONE), kv_out)
    gather_kb = Gather(p, kvb, KV_FIRST, sems(KB_AT, GATHER_TWO))
    scatter = lambda base, parts, first, *bufs: Scatter(
        "tile", p.x, p.z, lane_devices, parts, first, bufs, sems(base, SUM_TWO if len(bufs) > 3 else SUM_ONE))
    head_scatter = lambda base, parts, *bufs: Scatter(
        "head", hy, hz, head_devices, parts, ROWS, bufs, sems(base, SUM_ONE))
    sum_da = Scatter("tile", 0, 0, lane_devices, d_parts.at[0], ROWS, (da_far, da_near, da_last), sems(DA_AT, SUM_ONE))
    sum_db = Scatter("tile", 0, 0, lane_devices, d_parts.at[1], DKV_FIRST,
                     (db_far, db_near, db_last, db_zed, db_far_b, db_near_b), sems(DB_AT, SUM_TWO))
    sum_gk = scatter(W_AT, gk_parts, KVW_FIRST, gk_far, gk_near, gk_last, gk_zed, gk_far_b, gk_near_b)
    sum_gq = scatter(O_AT, gq_parts, SUM_FIRST, gq_far, gq_near, gq_last, gq_zed, gq_far_b, gq_near_b)
    sum_go = scatter(GO_AT, go_parts, SUM_FIRST, go_far, go_near, go_last, go_zed, go_far_b, go_near_b)
    sum_out = head_scatter(OUT_AT, ho_parts, ho_far, ho_near, ho_last)
    sum_tok = head_scatter(TOK_AT, ht_parts, ht_far, ht_near, ht_last)

    loads[0].wait()
    gather_w.start()

    height = lax.rem(slab[p.me], 4)
    near_height = lax.rem(slab[p.sib], 4)
    far_height = lax.rem(slab[at_tile(p.z, p.xr, 1 - p.c)], 4)
    key_width = lax.broadcasted_iota(jnp.int32, (64, ROWS), 1) // 64
    for qw in range(4):
        reach_h = ext[0, height * 4 + qw]
        reach_w = ext[1, height * 4 + qw]
        near_w = jnp.where(jnp.abs(key_width - qw) <= reach_w, 1.0, 0.0)
        for m, other in enumerate((height, near_height, far_height)):
            gap = jnp.full((64, ROWS), jnp.abs(height - other), jnp.int32)
            mask[m, qw * 64:(qw + 1) * 64] = jnp.where(gap <= reach_h, near_w, 0.0)

    loads[2].wait()
    loads[3].wait()

    def turn(src, dst):
        def body(j, carry):
            cols = pl.ds(pl.multiple_of(j * 384, 384), 384)
            dst[j] = src[:, cols].T.reshape(2, OWN, ROWS)
            return carry
        lax.fori_loop(0, 8, body, 0)

    turn(tok, tok_t)
    tok_swap = to_sibling(0, tok_t.at[:, 1 - p.c], tok_sib)
    turn(cot, cot_t)
    cot_swap = to_sibling(1, cot_t.at[:, 1 - p.c], cot_sib)

    def project(z, x):
        j = z * 4 + x
        t = tok[:, pl.ds(pl.multiple_of(j * 384, 384), 384)]

        def one(i, carry):
            rows = pl.ds(pl.multiple_of(i * OWN, OWN), OWN)
            proj[i] += dot(t, w[pl.ds(2 * j, 2), rows, :].reshape(2 * OWN, WID))
            return carry
        lax.fori_loop(0, 3, one, 0)

    proj[...] = jnp.zeros_like(proj)
    gather_w.start_rest(True)
    gather_w.step_across()
    gather_w.sib_own()
    project(p.z, p.x)
    gather_w.step_sides()
    loads[1].wait()
    gather_o.start()
    gather_o.start_rest(False)
    gather_w.sib_sides()
    project(p.z, p.xl)
    project(p.z, p.xr)
    gather_w.step_sides_across()
    gather_o.step_across()
    gather_w.sib_across()
    project(1 - p.z, p.x)
    gather_w.step_opposite()
    gather_w.sib_sides_across()
    project(1 - p.z, p.xl)
    project(1 - p.z, p.xr)
    gather_w.step_last()
    gather_o.step_sides()
    gather_w.sib_opposite()
    project(p.z, p.xo)
    gather_w.sib_last()
    project(1 - p.z, p.xo)

    def scale_of(raw):
        return lax.rsqrt(jnp.mean(raw * raw, axis=-1, keepdims=True) + EPS)

    def head_of(of, i):
        return of(lambda cols: proj[i, :, cols])

    def unit_rows(of, i):
        raw = head_of(of, i)
        return (raw * scale_of(raw)).astype(BF)

    kv_out[:, :HD] = unit_rows(of_x, 1)
    kv_out[:, HD:] = head_of(of_x, 2).astype(BF)
    kva[p.me, :, :HD] = unit_rows(of_a, 1)
    kva[p.me, :, HD:] = head_of(of_a, 2).astype(BF)
    gather_ka.start()
    kvb[p.me, :, :HD] = unit_rows(of_b, 1)
    kvb[p.me, :, HD:] = head_of(of_b, 2).astype(BF)
    gather_kb.start()
    pair_out[0] = unit_rows(of_x, 0)
    q_pair = to_across(0, q.at[1])
    gather_kb.start_rest(False)
    q[0] = unit_rows(of_a, 0)
    q[2] = unit_rows(of_b, 0)
    for u in (0, 2):
        qt[u] = q[u].T

    def block(fn, *args):
        pl.when(p.me >= 0)(lambda: fn(*args))

    def forward(t, m, i, units=(0, 1, 2), first=False):
        block(forward_block, t, m, i, units, first)

    def forward_block(t, m, i, units, first):
        for u in units:
            kv = kva if u < 2 else kvb
            scores = dot_nt(q[u], kv[t, :, :HD])
            we = jnp.exp2(scores * EXP2_SCALE) * mask[m]
            wexp[i, u] = we
            part = we[:, :HD] + we[:, HD:]
            val = dot(we.astype(BF), kv[t, :, HD:])
            if first:
                den[u] = part
                num[u] = val
            else:
                den[u] += part
                num[u] += val

    def loop2(fn):
        lax.fori_loop(0, 2, lambda i, carry: (fn(i), carry)[1], 0)

    def grad_att(j, acc):
        cols = pl.ds(pl.multiple_of(j * 384, 384), 384)
        return acc + dot(cot[:, cols], wo[pl.ds(2 * j, 2)].reshape(2 * OWN, WID))

    def two(first, second):
        forward(*first)
        forward(*second)

    def side(zz, i):
        two((at_tile(zz, p.xl, 1 - p.c), 2, 4 + 2 * i), (at_tile(zz, p.xr, 1 - p.c), 2, 5 + 2 * i))

    forward(p.me, 0, 0, (0, 2), True)
    gather_o.step_sides_across()
    gather_ka.step_across()
    gather_kb.step_across()
    gather_o.step_opposite()
    gather_ka.sib_own()
    gather_kb.sib_own()
    q_pair.wait_recv()
    qt[1] = q[1].T
    forward(p.me, 0, 0, (1,), True)
    forward(p.sib, 1, 2)
    gather_kb.step_sides()
    gather_ka.step_sides()
    gather_ka.step_sides_across()
    gather_kb.step_sides_across()
    forward(p.across, 0, 1)
    gather_o.step_last()
    gather_ka.sib_sides()
    gather_kb.sib_sides()
    side(p.z, 0)
    gather_ka.step_opposite()
    gather_kb.step_opposite()
    gather_ka.sib_across()
    gather_kb.sib_across()
    two((at_tile(1 - p.z, p.x, 1 - p.c), 1, 3), (at_tile(p.z, p.xo, p.c), 0, 8))
    gather_o.sib_own()
    gather_o.sib_across()
    gather_o.sib_sides()
    gather_o.sib_sides_across()
    gather_o.sib_opposite()
    gather_o.sib_last()
    g_all[...] = lax.fori_loop(0, 8, grad_att, jnp.zeros((ROWS, WID), F32)).astype(BF)
    pair_out[1] = of_x(lambda cols: g_all[:, cols])
    g_pair = to_across(1, g.at[1])
    gather_ka.step_last()
    gather_kb.step_last()
    gather_ka.sib_sides_across()
    gather_kb.sib_sides_across()
    side(1 - p.z, 1)
    g[0] = of_a(lambda cols: g_all[:, cols])
    g[2] = of_b(lambda cols: g_all[:, cols])
    for u in (0, 2):
        gt[u] = g[u].T
    gather_ka.sib_opposite()
    gather_kb.sib_opposite()
    two((at_tile(p.z, p.xo, 1 - p.c), 1, 10), (at_tile(1 - p.z, p.xo, p.c), 0, 9))
    gather_ka.sib_last()
    gather_kb.sib_last()
    forward(at_tile(1 - p.z, p.xo, 1 - p.c), 1, 11)
    g_pair.wait_recv()
    gt[1] = g[1].T

    for u in (1, 0, 2):
        inverse = 1.0 / jnp.sum(den[u], axis=-1, keepdims=True)
        context = num[u] * inverse
        if u == 1:
            pair_out[2] = context.astype(BF)
            att_pair = to_across(2, pair_in.at[0])
        else:
            att[0, head_a if u == 0 else 1] = context.astype(BF)
        row = jnp.sum(g[u].astype(F32) * context, axis=-1, keepdims=True)
        delta[u] = jnp.broadcast_to(row, (ROWS, HD))
        den[u] = jnp.broadcast_to(inverse, (ROWS, HD))

    def backward(t, i, x, z, own):
        block(backward_block, t, i, x, z, own)

    def backward_block(t, i, x, z, own):
        dk, dv = [], []
        for u in range(NH):
            kv = kva if u < 2 else kvb
            grad = dot_nt(g[u], kv[t, :, HD:])
            inverse, row = den[u], delta[u]
            probs, ds = [], []
            for part in range(2):
                cs = slice(part * HD, (part + 1) * HD)
                pr = wexp[i, u, :, cs] * inverse
                ds.append((pr * (grad[:, cs] - row)).astype(BF))
                probs.append(pr.astype(BF))
            probs = jnp.concatenate(probs, axis=1)
            ds = jnp.concatenate(ds, axis=1)
            dq[u] += dot(ds, kv[t, :, :HD])
            dk.append(dot(qt[u], ds))
            dv.append(dot(gt[u], probs))
        for n, ks, vs in ((0, dk[0] + dk[1], dv[0] + dv[1]), (1, dk[2], dv[2])):
            ks = ks * INV_ROOT
            if own:
                ks = ks + d_parts[n, x, z, :HD].astype(F32)
                vs = vs + d_parts[n, x, z, HD:].astype(F32)
            out = d_parts if own else d_out
            out[n, x, z, :HD] = ks.astype(BF)
            out[n, x, z, HD:] = vs.astype(BF)

    def swap_copy(x, z, k):
        return pltpu.make_async_remote_copy(
            src_ref=d_out.at[:, x, z], dst_ref=d_parts.at[:, x, z], send_sem=dkv_send.at[k], recv_sem=dkv_recv.at[k],
            device_id={"tile": p.sib}, device_id_type=MESH)

    def swap(x, z, k):
        c = swap_copy(x, z, k)
        c.start()
        sent.append(c)

    def swapped(x, z, k):
        swap_copy(x, z, k).wait_recv()

    def out_part(ring):
        def one(i):
            o = wo[pl.ds(4 * ring + 2 * i, 2)].reshape(2 * OWN, WID)
            ho_parts[ring, i] = dot_nt(wide(att, 0), o).astype(BF)
        loop2(one)

    def tok_part(ring):
        def one(i):
            j = 2 * ring + i
            acc = dot_nt(wide(gp, 0, 0), w[pl.ds(2 * j, 2), 0:OWN, :].reshape(2 * OWN, WID))
            for n in range(1, 3):
                acc += dot_nt(wide(gp, 0, n), w[pl.ds(2 * j, 2), n * OWN:(n + 1) * OWN, :].reshape(2 * OWN, WID))
            ht_parts[ring, i] = acc.astype(BF)
        loop2(one)

    def out_grad(ring):
        def one(i):
            j = 4 * i + ring
            go_parts[ring, i] = (dot(cot_t[j, p.c], wide(att, 0)) + dot(cot_sib[j], wide(att, 1))).astype(BF)
        loop2(one)

    def qkv_grad(parts, j, which):
        for n, i in enumerate(which):
            parts[j % 4, j // 4, n * OWN:(n + 1) * OWN] = (
                dot(tok_t[j, p.c], wide(gp, 0, i)) + dot(tok_sib[j], wide(gp, 1, i))).astype(BF)

    def kv_grad(ring):
        loop2(lambda i: qkv_grad(gk_parts, i * 4 + ring, (1, 2)))

    def opposite_sib(i):
        zz = (p.z + i) % 2
        backward(at_tile(zz, p.xo, 1 - p.c), 10 + i, 2, i, False)

    def opposite_own(i):
        zz = (p.z + i) % 2
        backward(at_tile(zz, p.xo, p.c), 8 + i, 2, i, True)

    def sides_sib(i):
        zz = (p.z + 1 + i) % 2
        backward(at_tile(zz, p.xl, 1 - p.c), 6 - 2 * i, 3, 1 - i, False)
        backward(at_tile(zz, p.xr, 1 - p.c), 7 - 2 * i, 1, 1 - i, False)

    def own_sib(i):
        zz = (p.z + i) % 2
        backward(at_tile(zz, p.x, 1 - p.c), 2 + i, 0, i, False)

    def own_own(i):
        zz = (p.z + i) % 2
        backward(at_tile(zz, p.x, p.c), i, 0, i, True)

    def unit_back(grad, raw):
        scale = scale_of(raw)
        unit = raw * scale
        return scale * (grad - unit * jnp.mean(grad * unit, axis=-1, keepdims=True))

    dq[...] = jnp.zeros_like(dq)
    opposite_sib(1)
    swap(2, 1, 0)
    opposite_sib(0)
    swap(2, 0, 1)
    swapped(2, 1, 0)
    opposite_own(1)
    sum_da.start_far(0)
    sum_db.start_far(0)
    swapped(2, 0, 1)
    opposite_own(0)
    sum_da.start_far(1)
    sum_db.start_far(1)
    att_pair.wait_recv()
    att[0, head_x] = pair_in[0]
    att_swap = to_sibling(2, att.at[0], att.at[1])
    sides_sib(0)
    swap(3, 1, 2)
    swap(1, 1, 3)
    cot_swap.wait_recv()
    att_swap.wait_recv()
    out_grad(p.xo)
    sum_go.start_far(0, False)
    sum_go.start_far(1, False)
    sides_sib(1)
    swap(3, 0, 4)
    swap(1, 0, 5)
    out_part(sum_out.ro)
    sum_out.start_far(0)
    sum_out.start_far(1)
    swapped(3, 1, 2)
    swapped(1, 1, 3)
    sum_da.start_near(0)
    sum_db.start_near(0)
    out_part(sum_out.rr)
    out_part(sum_out.rl)
    sum_out.start_near(0)
    sum_out.start_near(1)
    swapped(3, 0, 4)
    swapped(1, 0, 5)
    sum_da.start_near(1)
    sum_db.start_near(1)
    sum_da.step_near(0)
    sum_db.step_far_b()
    out_grad(p.xr)
    out_grad(p.xl)
    sum_go.start_z(0, p.xo)
    sum_go.start_z(1, p.xr)
    sum_go.start_z(2, p.xl)
    loop2(own_sib)
    swap(0, 0, 6)
    swap(0, 1, 7)
    sum_db.step_near(0)
    sum_da.step_near(1)
    sum_db.step_near(1)
    swapped(0, 0, 6)
    swapped(0, 1, 7)
    loop2(own_own)
    sum_db.start_own()
    pair_out[3] = dq[1].astype(BF)
    dq_pair = to_across(3, pair_in.at[1])
    out_grad(p.x)
    sum_db.step_near_b()
    sum_go.start_near(0, False)
    sum_go.start_near(1, False)
    sum_go.step_near(0)
    sum_go.step_near(1)
    sum_go.start_own()
    out_part(sum_out.ring)
    sum_da.step_pair()
    sum_db.step_pair()

    def head_grad(i, of, head, grad):
        gp[0, i, head] = unit_back(grad, head_of(of, i)).astype(BF)

    head_grad(0, of_a, head_a, dq[0] * INV_ROOT)
    head_grad(0, of_b, 1, dq[2] * INV_ROOT)
    dq_pair.wait_recv()
    head_grad(0, of_x, head_x, pair_in[1].astype(F32) * INV_ROOT)
    gq_swap = to_sibling(3, gp.at[0, 0], gp.at[1, 0])
    sum_out.step_near(0)
    sum_out.step_near(1)

    tok_swap.wait_recv()
    gq_swap.wait_recv()
    lax.fori_loop(0, 8, lambda j, carry: (qkv_grad(gq_parts, j, (0,)), carry)[1], 0)
    gather_w.finish()
    gather_o.finish()
    sum_gq.start_far(0, False)
    sum_gq.start_far(1, False)
    sum_gq.start_near(0, False)
    sum_gq.start_near(1, False)
    sum_gq.start_over()

    def kv_head(n, of, head):
        head_grad(1, of, head, dkv_sum[n, :HD].T)
        gp[0, 2, head] = dkv_sum[n, HD:].T.astype(BF)

    sum_da.result_own(dkv_sum.at[0])
    kv_head(0, of_a, head_a)
    sum_db.result_b(dkv_sum.at[1])
    sum_db.result_a(dkv_sum.at[1])
    kv_head(1, of_b, 1)
    sum_da.result_last(dkv_sum.at[2])
    kv_head(2, of_x, head_x)
    gk_swap = to_sibling(4, gp.at[0, pl.ds(1, 2)], gp.at[1, pl.ds(1, 2)])

    sum_out.step_pair()
    sum_go.step_far_b()
    tok_part(sum_tok.ro)
    sum_tok.start_far(0)
    sum_tok.start_far(1)
    gk_swap.wait_recv()
    kv_grad(p.xo)
    sum_gk.start_far(0)
    sum_gk.start_far(1)
    sum_go.step_pair()
    sum_gq.step_near(0)
    sum_gq.step_near(1)
    sum_go.step_near_b()
    tok_part(sum_tok.rr)
    tok_part(sum_tok.rl)
    sum_tok.start_near(0)
    sum_tok.start_near(1)
    kv_grad(p.xr)
    kv_grad(p.xl)
    sum_gk.start_near(0)
    sum_gk.start_near(1)
    sum_gq.step_far_b()
    tok_part(sum_tok.ring)
    sum_tok.step_near(0)
    sum_tok.step_near(1)
    kv_grad(p.x)
    sum_gk.start_own()
    sum_gk.step_near(0)
    sum_gk.step_near(1)
    sum_gk.step_far_b()
    sum_gq.step_near_b()
    sum_out.result_a(out_ref)
    sum_go.result_b(gout_ref)
    sum_go.result_a(gout_ref)
    sum_tok.step_pair()
    sum_gq.step_pair()
    sum_gk.step_near_b()
    sum_gk.step_pair()
    sum_gq.result_b(gqkv_ref.at[pl.ds(0, OWN)])
    sum_gq.result_a(gqkv_ref.at[pl.ds(0, OWN)])
    sum_tok.result_a(gtok_ref)
    sum_gk.result_b(gqkv_ref.at[pl.ds(OWN, 2 * OWN)])
    sum_gk.result_a(gqkv_ref.at[pl.ds(OWN, 2 * OWN)])

    for s in (gather_ka, gather_kb, sum_da, sum_db, sum_gq, sum_gk, sum_go, sum_out, sum_tok):
        s.finish()
    for c in sent:
        c.wait_send()


def lane_bufs(rows, first, cols):
    _, ah, _, bh = split_rows(rows, first)
    second = rows - first
    bufs = [(2, 2, ah[0].size, cols), (2, 2, first, cols), (first, cols)]
    if second:
        bufs += [(4, second, cols), (2, bh[1].size, cols), (2, second, cols)]
    return [pltpu.VMEM(b, BF) for b in bufs]


def deliver(*refs):
    for i in range(4):
        refs[4 + i][...] = refs[i][...]


def local(tokens, cotangent, qkv_weight, out_weight, slab_of_device, extents):
    w = jnp.transpose(qkv_weight, (1, 0, 2)).reshape(3 * OWN, WID)
    vm = lambda *shape, dtype=BF: pltpu.VMEM(shape, dtype)
    dma = lambda *shape: pltpu.SemaphoreType.DMA(shape)
    scratch = [
        vm(16, 3 * OWN, WID), vm(16, OWN, WID), vm(16, ROWS, ROWS), vm(16, ROWS, ROWS), vm(ROWS, ROWS), vm(ROWS, D), vm(ROWS, D),
        vm(8, 2, OWN, ROWS), vm(8, OWN, ROWS), vm(8, 2, OWN, ROWS), vm(8, OWN, ROWS),
        vm(12, NH, ROWS, ROWS, dtype=F32), vm(3, ROWS, ROWS, dtype=F32),
        vm(3, ROWS, WID, dtype=F32), vm(NH, ROWS, HD), vm(NH, HD, ROWS),
        vm(ROWS, WID), vm(NH, ROWS, HD), vm(NH, HD, ROWS),
        vm(NH, ROWS, HD, dtype=F32), vm(NH, ROWS, HD, dtype=F32), vm(NH, ROWS, HD, dtype=F32),
        vm(NH, ROWS, HD, dtype=F32), vm(2, NH, ROWS, HD), vm(2, 3, NH, ROWS, HD), vm(NH, ROWS, ROWS, dtype=F32),
        vm(4, ROWS, HD), vm(2, ROWS, HD),
        vm(2, 4, 2, ROWS, ROWS), vm(2, 4, 2, ROWS, ROWS),
        *lane_bufs(ROWS, ROWS, ROWS), *lane_bufs(ROWS, DKV_FIRST, ROWS),
        vm(4, 2, OWN, WID), *lane_bufs(OWN, SUM_FIRST, WID),
        vm(4, 2, 2 * OWN, WID), *lane_bufs(2 * OWN, KVW_FIRST, WID),
        vm(4, 2, OWN, WID), *lane_bufs(OWN, SUM_FIRST, WID),
        vm(4, 2, ROWS, WID), *lane_bufs(ROWS, ROWS, WID), vm(4, 2, ROWS, WID), *lane_bufs(ROWS, ROWS, WID),
        dma(4), dma(SEMS), dma(SEMS), dma(5), dma(5), dma(8), dma(8), dma(4), dma(4),
    ]
    any_spec = pl.BlockSpec(memory_space=pl.ANY)
    smem = pl.BlockSpec(memory_space=pltpu.SMEM)
    vmem = pl.BlockSpec(memory_space=pltpu.VMEM)
    shapes = (
        jax.ShapeDtypeStruct((ROWS, WID), BF), jax.ShapeDtypeStruct((ROWS, WID), BF),
        jax.ShapeDtypeStruct((3 * OWN, WID), F32), jax.ShapeDtypeStruct((OWN, WID), F32))
    results = pl.pallas_call(
        kernel,
        out_shape=shapes,
        in_specs=[any_spec] * 4 + [smem] * 2,
        out_specs=(vmem,) * 4,
        scratch_shapes=scratch,
        compiler_params=pltpu.CompilerParams(
            collective_id=0, has_side_effects=True, vmem_limit_bytes=64 * 1024 * 1024),
        cost_estimate=pl.CostEstimate(flops=20_000_000_000, bytes_accessed=10_000_000, transcendentals=2_400_000),
        name="sublayer",
    )(tokens, cotangent, w, out_weight, slab_of_device, extents.T)
    output, grad_tokens, grad_qkv, grad_out = pl.pallas_call(
        deliver, out_shape=shapes, in_specs=[vmem] * 4, out_specs=(vmem,) * 4, name="deliver")(*results)
    grad_qkv = jnp.transpose(grad_qkv.reshape(3, OWN, WID), (1, 0, 2))
    return output, grad_tokens, grad_qkv, grad_out


def solution(mesh):
    return jax.shard_map(
        local, mesh=mesh,
        in_specs=(P("tile", None), P("tile", None), P("tile", None, "head"), P("tile", "head"), P(None), P(None, None)),
        out_specs=(P("tile", "head"), P("tile", "head"), P("tile", None, "head"), P("tile", "head")),
        check_vma=False)
```

```python
import math

import jax
import jax.numpy as jnp
from jax import lax
from jax.experimental import pallas as pl
from jax.experimental.pallas import tpu as pltpu
from jax.sharding import PartitionSpec as P

MESH = pl.DeviceIdType.MESH
HD = 128
NH = 3
ROWS = 256
WID = NH * HD
D = 3072
OWN = 192
EPS = 1e-06
INV_ROOT = 1.0 / math.sqrt(HD)
EXP2_SCALE = INV_ROOT * math.log2(math.e)
BF = jnp.bfloat16
F32 = jnp.float32
GATHER_TWO, GATHER_ONE = range(31), (0, 3, 4, 6, 7, 8, 9, 14, 15, 18, 19, 21, 22, 23, 24, 26, 29)
SUM_TWO, SUM_ONE = range(23), (*range(4, 16), 22)
W_AT, O_AT, KB_AT, KA_AT, DB_AT, GO_AT, DA_AT, OUT_AT, TOK_AT, SEMS = 0, 31, 62, 93, 110, 133, 156, 169, 182, 195
SUM_FIRST = 144
QKV_FIRST, OUT_FIRST, KV_FIRST, DKV_FIRST, KVW_FIRST = 320, 112, 64, 64, 304


def dot(a, b):
    return jnp.dot(a, b, preferred_element_type=F32)


def dot_nt(a, b):
    return lax.dot_general(a, b, (((1,), (1,)), ((), ())), preferred_element_type=F32)


def at_tile(z, x, c):
    return z * 8 + x * 2 + c


class Place:
    def __init__(self):
        t = lax.axis_index("tile")
        self.me = t
        self.z, self.x, self.c = t // 8, (t // 2) % 4, t % 2
        self.xr, self.xl, self.xo = (self.x + 1) % 4, (self.x + 3) % 4, (self.x + 2) % 4
        self.right = at_tile(self.z, self.xr, self.c)
        self.left = at_tile(self.z, self.xl, self.c)
        self.across = at_tile(1 - self.z, self.x, self.c)
        self.sib = at_tile(self.z, self.x, 1 - self.c)


def split_rows(rows, first):
    def halves(start, size, up):
        half = size // 32 * 16 + (16 if up and size % 32 else 0)
        return pl.ds(start, size), (pl.ds(start, half), pl.ds(start + half, size - half))
    a, ah = halves(0, first, True)
    b, bh = halves(first, rows - first, False)
    return a, ah, b, bh


class Sems:
    def __init__(self, send, recv, base, keys):
        self.send, self.recv, self.base, self.keys = send, recv, base, tuple(keys)

    def __call__(self, k):
        i = self.base + self.keys.index(k)
        return dict(send_sem=self.send.at[i], recv_sem=self.recv.at[i])


class Gather:
    def __init__(self, place, buf, first, sems, for_across=None):
        self.p, self.buf, self.sems = place, buf, sems
        self.two, self.for_across = first < buf.shape[1], for_across
        self.a, self.ah, self.b, self.bh = split_rows(buf.shape[1], first)
        self.sent = []

    def copy(self, k, ref, dev):
        return pltpu.make_async_remote_copy(
            src_ref=ref, dst_ref=ref, **self.sems(k), device_id={"tile": dev}, device_id_type=MESH)

    def go(self, k, t, rows, dev):
        c = self.copy(k, self.buf.at[t, rows], dev)
        c.start()
        self.sent.append(c)

    def got(self, k, t, rows):
        self.copy(k, self.buf.at[t, rows], self.p.sib).wait_recv()

    def start(self):
        p = self.p
        if self.two:
            self.go(0, p.me, self.a, p.across)
            self.go(1, p.me, self.b, p.right)
            self.go(2, p.me, self.b, p.left)
        else:
            c = pltpu.make_async_remote_copy(
                src_ref=self.for_across, dst_ref=self.buf.at[p.me], **self.sems(0),
                device_id={"tile": p.across}, device_id_type=MESH)
            c.start()
            self.sent.append(c)
            self.go(3, p.me, self.a, p.right)
            self.go(4, p.me, self.a, p.left)
        c = self.copy(6, self.buf.at[p.me], p.sib)
        c.start()
        self.sent.append(c)

    def start_rest(self, in_turn):
        p = self.p
        if in_turn:
            for c in self.sent[1:3]:
                c.wait_send()
        self.go(3, p.me, self.a, p.right)
        self.go(4, p.me, self.a, p.left)
        if in_turn:
            self.sent[0].wait_send()
            del self.sent[:3]
        self.go(5, p.me, self.b, p.across)

    def step_across(self):
        p = self.p
        self.got(0, p.across, self.a)
        self.go(7, p.across, self.a, p.right)
        self.go(8, p.across, self.a, p.left)
        self.go(9, p.across, self.a, p.sib)

    def step_sides(self):
        p = self.p
        if self.two:
            self.got(1, p.left, self.b)
            self.go(10, p.left, self.bh[0], p.right)
            self.go(11, p.left, self.b, p.across)
            self.got(2, p.right, self.b)
            self.go(12, p.right, self.bh[1], p.left)
            self.go(13, p.right, self.b, p.across)
        self.got(3, p.left, self.a)
        self.go(14, p.left, self.ah[0], p.right)
        self.got(4, p.right, self.a)
        self.go(15, p.right, self.ah[1], p.left)
        if self.two:
            self.go(16, p.left, self.b, p.sib)
            self.go(17, p.right, self.b, p.sib)
        self.go(18, p.left, self.a, p.sib)
        self.go(19, p.right, self.a, p.sib)

    def step_sides_across(self):
        p = self.p
        zl, zr = at_tile(1 - p.z, p.xl, p.c), at_tile(1 - p.z, p.xr, p.c)
        to = at_tile(p.z, p.xo, p.c)
        if self.two:
            self.got(10, to, self.bh[0])
            self.got(12, to, self.bh[1])
            self.go(25, to, self.b, p.across)
        self.got(7, zl, self.a)
        self.go(21, zl, self.ah[0], p.right)
        self.got(8, zr, self.a)
        self.go(22, zr, self.ah[1], p.left)
        self.go(23, zl, self.a, p.sib)
        self.go(24, zr, self.a, p.sib)
        if self.two:
            self.got(5, p.across, self.b)
            self.go(20, p.across, self.b, p.sib)

    def step_opposite(self):
        p = self.p
        zl, zr = at_tile(1 - p.z, p.xl, p.c), at_tile(1 - p.z, p.xr, p.c)
        to = at_tile(p.z, p.xo, p.c)
        self.got(14, to, self.ah[0])
        self.got(15, to, self.ah[1])
        c = self.copy(26, self.buf.at[to], p.sib)
        c.start()
        self.sent.append(c)
        if self.two:
            self.got(11, zl, self.b)
            self.go(27, zl, self.b, p.sib)
            self.got(13, zr, self.b)
            self.go(28, zr, self.b, p.sib)

    def step_last(self):
        p = self.p
        zo = at_tile(1 - p.z, p.xo, p.c)
        self.got(21, zo, self.ah[0])
        self.got(22, zo, self.ah[1])
        self.go(29, zo, self.a, p.sib)
        if self.two:
            self.got(25, zo, self.b)
            self.go(30, zo, self.b, p.sib)

    def sib_own(self):
        self.copy(6, self.buf.at[self.p.sib], self.p.sib).wait_recv()

    def sib_across(self):
        p = self.p
        t = at_tile(1 - p.z, p.x, 1 - p.c)
        self.got(9, t, self.a)
        if self.two:
            self.got(20, t, self.b)

    def sib_sides(self):
        p = self.p
        tl, tr = at_tile(p.z, p.xl, 1 - p.c), at_tile(p.z, p.xr, 1 - p.c)
        if self.two:
            self.got(16, tl, self.b)
            self.got(17, tr, self.b)
        self.got(18, tl, self.a)
        self.got(19, tr, self.a)

    def sib_sides_across(self):
        p = self.p
        zl, zr = at_tile(1 - p.z, p.xl, 1 - p.c), at_tile(1 - p.z, p.xr, 1 - p.c)
        self.got(23, zl, self.a)
        self.got(24, zr, self.a)
        if self.two:
            self.got(27, zl, self.b)
            self.got(28, zr, self.b)

    def sib_opposite(self):
        p = self.p
        self.copy(26, self.buf.at[at_tile(p.z, p.xo, 1 - p.c)], p.sib).wait_recv()

    def sib_last(self):
        p = self.p
        zo = at_tile(1 - p.z, p.xo, 1 - p.c)
        self.got(29, zo, self.a)
        if self.two:
            self.got(30, zo, self.b)

    def finish(self):
        for c in self.sent:
            c.wait_send()


class Scatter:
    def __init__(self, axis, ring, pair, devices, parts, first, bufs, sems):
        self.axis, self.ring, self.pair = axis, ring, pair
        self.right, self.left, self.across = devices
        self.parts = parts
        self.far, self.near, self.last = bufs[:3]
        self.zed, self.far_b, self.near_b = bufs[3:] if len(bufs) > 3 else (None, None, None)
        self.sems = sems
        self.rr, self.rl, self.ro = (ring + 1) % 4, (ring + 3) % 4, (ring + 2) % 4
        self.a, self.ah, self.b, self.bh = split_rows(parts.shape[2], first)
        self.first = first
        self.bl = [pl.ds(h.start - first, h.size) for h in self.bh]
        self.sent = []

    def copy(self, k, src, dst, dev):
        return pltpu.make_async_remote_copy(
            src_ref=src, dst_ref=dst, **self.sems(k), device_id={self.axis: dev}, device_id_type=MESH)

    def go(self, k, src, dst, dev):
        c = self.copy(k, src, dst, dev)
        c.start()
        self.sent.append(c)

    def got(self, k, dst):
        self.copy(k, dst, dst, self.right).wait_recv()

    def add(self, ring, pair, rows, got):
        self.parts[ring, pair, rows] = (
            self.parts[ring, pair, rows].astype(F32) + got.astype(F32)).astype(BF)


    def pairs(self):
        return (0, 1 - self.pair), (1, self.pair)

    def start_z(self, k, ring):
        if self.zed is not None:
            self.go(k, self.parts.at[ring, 1 - self.pair, self.b], self.zed.at[ring], self.across)

    def got_z(self, k, ring):
        self.got(k, self.zed.at[ring])

    def far_at(self, i, n):
        return self.far.at[i, n, pl.ds(0, self.ah[i].size)]

    def start_far(self, n, over=True):
        z = self.pairs()[n][1]
        for i, dev in enumerate((self.right, self.left)):
            self.go(4 + 2 * n + i, self.parts.at[self.ro, z, self.ah[i]], self.far_at(i, n), dev)
        if n == 0 and over:
            self.start_z(0, self.ro)

    def start_near(self, n, over=True):
        z = self.pairs()[n][1]
        for i, (ring, dev) in enumerate(((self.rr, self.right), (self.rl, self.left))):
            rows = self.ah[1 - i]
            self.go(8 + 2 * n + i, self.parts.at[ring, z, rows], self.near.at[i, n, rows], dev)
            if n == 0 and over:
                self.start_z(1 + i, ring)

    def start_own(self):
        self.start_z(3, self.ring)

    def start_over(self):
        for k, ring in enumerate((self.ro, self.rr, self.rl, self.ring)):
            self.start_z(k, ring)

    def step_far_b(self):
        self.got_z(0, self.ro)
        self.add(self.ro, self.pair, self.b, self.zed[self.ro])
        for i, dev in enumerate((self.right, self.left)):
            self.go(16 + i, self.parts.at[self.ro, self.pair, self.bh[i]], self.far_b.at[i, pl.ds(0, self.bh[i].size)], dev)

    def step_near(self, n):
        z = self.pairs()[n][1]
        for i, (ring, dev) in enumerate(((self.rr, self.right), (self.rl, self.left))):
            rows, got = self.ah[i], self.far_at(i, n)
            self.got(4 + 2 * n + i, got)
            self.add(ring, z, rows, got[...])
            self.go(12 + 2 * n + i, self.parts.at[ring, z, rows], self.near.at[i, n, rows], dev)

    def step_near_b(self):
        for i, (ring, dev) in enumerate(((self.rr, self.right), (self.rl, self.left))):
            self.got_z(1 + i, ring)
            self.add(ring, self.pair, self.b, self.zed[ring])
            j = 1 - i
            self.go(18 + i, self.parts.at[ring, self.pair, self.bh[j]], self.near_b.at[i, self.bl[j]], dev)
        for i, (ring, dev) in enumerate(((self.rr, self.right), (self.rl, self.left))):
            got = self.far_b.at[i, pl.ds(0, self.bh[i].size)]
            self.got(16 + i, got)
            self.add(ring, self.pair, self.bh[i], got[...])
            self.go(20 + i, self.parts.at[ring, self.pair, self.bh[i]], self.near_b.at[i, self.bl[i]], dev)

    def total(self, n):
        for i in range(2):
            self.got(8 + 2 * n + i, self.near.at[i, n, self.ah[1 - i]])
            self.got(12 + 2 * n + i, self.near.at[i, n, self.ah[i]])
        z = self.pairs()[n][1]
        return (self.parts[self.ring, z, self.a].astype(F32) + self.near[0, n].astype(F32)
                + self.near[1, n].astype(F32))

    def step_pair(self):
        other = 1 - self.pair
        self.parts[self.ring, other, self.a] = self.total(0).astype(BF)
        self.go(22, self.parts.at[self.ring, other, self.a], self.last, self.across)

    def result_b(self, out):
        self.got_z(3, self.ring)
        for i in range(2):
            self.got(18 + i, self.near_b.at[i, self.bl[1 - i]])
            self.got(20 + i, self.near_b.at[i, self.bl[i]])
        out[self.b] = (
            (self.parts[self.ring, self.pair, self.b].astype(F32) + self.zed[self.ring].astype(F32))
            + (self.near_b[0].astype(F32) + self.near_b[1].astype(F32))).astype(out.dtype)

    def result_own(self, out):
        out[...] = self.total(1)

    def result_last(self, out):
        self.got(22, self.last)
        out[...] = self.last[...].astype(F32)

    def result_a(self, out):
        own = self.total(1)
        self.got(22, self.last)
        out[self.a] = (own + self.last[...].astype(F32)).astype(out.dtype)

    def finish(self):
        for c in self.sent:
            c.wait_send()


def kernel(tok_hbm, cot_hbm, w_hbm, wo_hbm, slab, ext,
           out_ref, gtok_ref, gqkv_ref, gout_ref,
           w, wo, kva, kvb, kv_out, tok, cot, tok_t, tok_sib, cot_t, cot_sib, wexp, mask,
           proj, q, qt, g_all, g, gt, num, den, delta, dq, att, gp, dkv_sum, pair_out, pair_in,
           d_out, d_parts, da_far, da_near, da_last, db_far, db_near, db_last, db_zed, db_far_b, db_near_b,
           gq_parts, gq_far, gq_near, gq_last, gq_zed, gq_far_b, gq_near_b,
           gk_parts, gk_far, gk_near, gk_last, gk_zed, gk_far_b, gk_near_b,
           go_parts, go_far, go_near, go_last, go_zed, go_far_b, go_near_b,
           ho_parts, ho_far, ho_near, ho_last, ht_parts, ht_far, ht_near, ht_last,
           load_sem, lane_send, lane_recv, sib_send, sib_recv, dkv_send, dkv_recv, pair_send, pair_recv):
    p = Place()
    hd = lax.axis_index("head")
    hy, hz = hd // 2, hd % 2
    head_devices = (((hy + 1) % 4) * 2 + hz, ((hy + 3) % 4) * 2 + hz, hy * 2 + 1 - hz)
    lane_devices = (p.right, p.left, p.across)

    loads = [pltpu.make_async_copy(a, b, load_sem.at[i]) for i, (a, b) in enumerate((
        (w_hbm, w.at[p.me]), (wo_hbm, wo.at[p.me]), (tok_hbm, tok), (cot_hbm, cot)))]
    for c in loads:
        c.start()

    barrier = pltpu.get_barrier_semaphore()
    for dev in (p.right, p.left, p.across, p.sib):
        pl.semaphore_signal(barrier, inc=1, device_id={"tile": dev}, device_id_type=MESH)
    for dev in head_devices:
        pl.semaphore_signal(barrier, inc=1, device_id={"head": dev}, device_id_type=MESH)
    pl.semaphore_wait(barrier, 7)

    sent = []

    def to_sibling(k, src, dst):
        c = pltpu.make_async_remote_copy(
            src_ref=src, dst_ref=dst, send_sem=sib_send.at[k], recv_sem=sib_recv.at[k],
            device_id={"tile": p.sib}, device_id_type=MESH)
        c.start()
        sent.append(c)
        return c

    def sems(base, keys):
        return Sems(lane_send, lane_recv, base, keys)

    gather_w = Gather(p, w, QKV_FIRST, sems(W_AT, GATHER_TWO))
    gather_o = Gather(p, wo, OUT_FIRST, sems(O_AT, GATHER_TWO))
    head_a, head_x = 2 * p.z, 2 * (1 - p.z)
    row_0 = p.z == 0

    def of_a(get):
        return jnp.where(row_0, get(slice(0, HD)), get(slice(2 * HD, 3 * HD)))

    def of_x(get):
        return jnp.where(row_0, get(slice(2 * HD, 3 * HD)), get(slice(0, HD)))

    def of_b(get):
        return get(slice(HD, 2 * HD))

    def wide(ref, *index):
        return jnp.concatenate([ref[(*index, h)] for h in range(NH)], axis=1)

    def to_across(k, dst):
        c = pltpu.make_async_remote_copy(
            src_ref=pair_out.at[k], dst_ref=dst, send_sem=pair_send.at[k], recv_sem=pair_recv.at[k],
            device_id={"tile": p.across}, device_id_type=MESH)
        c.start()
        sent.append(c)
        return c

    gather_ka = Gather(p, kva, ROWS, sems(KA_AT, GATHER_ONE), kv_out)
    gather_kb = Gather(p, kvb, KV_FIRST, sems(KB_AT, GATHER_TWO))
    scatter = lambda base, parts, first, *bufs: Scatter(
        "tile", p.x, p.z, lane_devices, parts, first, bufs, sems(base, SUM_TWO if len(bufs) > 3 else SUM_ONE))
    head_scatter = lambda base, parts, *bufs: Scatter(
        "head", hy, hz, head_devices, parts, ROWS, bufs, sems(base, SUM_ONE))
    sum_da = Scatter("tile", 0, 0, lane_devices, d_parts.at[0], ROWS, (da_far, da_near, da_last), sems(DA_AT, SUM_ONE))
    sum_db = Scatter("tile", 0, 0, lane_devices, d_parts.at[1], DKV_FIRST,
                     (db_far, db_near, db_last, db_zed, db_far_b, db_near_b), sems(DB_AT, SUM_TWO))
    sum_gk = scatter(W_AT, gk_parts, KVW_FIRST, gk_far, gk_near, gk_last, gk_zed, gk_far_b, gk_near_b)
    sum_gq = scatter(O_AT, gq_parts, SUM_FIRST, gq_far, gq_near, gq_last, gq_zed, gq_far_b, gq_near_b)
    sum_go = scatter(GO_AT, go_parts, SUM_FIRST, go_far, go_near, go_last, go_zed, go_far_b, go_near_b)
    sum_out = head_scatter(OUT_AT, ho_parts, ho_far, ho_near, ho_last)
    sum_tok = head_scatter(TOK_AT, ht_parts, ht_far, ht_near, ht_last)

    loads[0].wait()
    gather_w.start()

    height = lax.rem(slab[p.me], 4)
    near_height = lax.rem(slab[p.sib], 4)
    far_height = lax.rem(slab[at_tile(p.z, p.xr, 1 - p.c)], 4)
    key_width = lax.broadcasted_iota(jnp.int32, (64, ROWS), 1) // 64
    for qw in range(4):
        reach_h = ext[0, height * 4 + qw]
        reach_w = ext[1, height * 4 + qw]
        near_w = jnp.where(jnp.abs(key_width - qw) <= reach_w, 1.0, 0.0)
        for m, other in enumerate((height, near_height, far_height)):
            gap = jnp.full((64, ROWS), jnp.abs(height - other), jnp.int32)
            mask[m, qw * 64:(qw + 1) * 64] = jnp.where(gap <= reach_h, near_w, 0.0)

    loads[2].wait()
    loads[3].wait()

    def turn(src, dst):
        def body(j, carry):
            cols = pl.ds(pl.multiple_of(j * 384, 384), 384)
            dst[j] = src[:, cols].T.reshape(2, OWN, ROWS)
            return carry
        lax.fori_loop(0, 8, body, 0)

    turn(tok, tok_t)
    tok_swap = to_sibling(0, tok_t.at[:, 1 - p.c], tok_sib)
    turn(cot, cot_t)
    cot_swap = to_sibling(1, cot_t.at[:, 1 - p.c], cot_sib)

    def project(z, x):
        j = z * 4 + x
        t = tok[:, pl.ds(pl.multiple_of(j * 384, 384), 384)]

        for i in range(3):
            proj[i] += dot(t, w[pl.ds(2 * j, 2), i * OWN:(i + 1) * OWN, :].reshape(2 * OWN, WID))

    proj[...] = jnp.zeros_like(proj)
    gather_w.start_rest(True)
    gather_w.step_across()
    gather_w.sib_own()
    project(p.z, p.x)
    gather_w.step_sides()
    loads[1].wait()
    gather_o.start()
    gather_o.start_rest(False)
    gather_w.sib_sides()
    project(p.z, p.xl)
    project(p.z, p.xr)
    gather_w.step_sides_across()
    gather_o.step_across()
    gather_w.sib_across()
    project(1 - p.z, p.x)
    gather_w.step_opposite()
    gather_w.sib_sides_across()
    project(1 - p.z, p.xl)
    project(1 - p.z, p.xr)
    gather_w.step_last()
    gather_o.step_sides()
    gather_w.sib_opposite()
    project(p.z, p.xo)
    gather_w.sib_last()
    project(1 - p.z, p.xo)

    def scale_of(raw):
        return lax.rsqrt(jnp.mean(raw * raw, axis=-1, keepdims=True) + EPS)

    def head_of(of, i):
        return of(lambda cols: proj[i, :, cols])

    def unit_rows(of, i):
        raw = head_of(of, i)
        return (raw * scale_of(raw)).astype(BF)

    kv_out[:, :HD] = unit_rows(of_x, 1)
    kv_out[:, HD:] = head_of(of_x, 2).astype(BF)
    kva[p.me, :, :HD] = unit_rows(of_a, 1)
    kva[p.me, :, HD:] = head_of(of_a, 2).astype(BF)
    gather_ka.start()
    kvb[p.me, :, :HD] = unit_rows(of_b, 1)
    kvb[p.me, :, HD:] = head_of(of_b, 2).astype(BF)
    gather_kb.start()
    pair_out[0] = unit_rows(of_x, 0)
    q_pair = to_across(0, q.at[1])
    gather_kb.start_rest(False)
    q[0] = unit_rows(of_a, 0)
    q[2] = unit_rows(of_b, 0)
    for u in (0, 2):
        qt[u] = q[u].T

    def block(fn, *args):
        pl.when(p.me >= 0)(lambda: fn(*args))

    def forward(t, m, i, units=(0, 1, 2), first=False):
        block(forward_block, t, m, i, units, first)

    def forward_block(t, m, i, units, first):
        for u in units:
            kv = kva if u < 2 else kvb
            scores = dot_nt(q[u], kv[t, :, :HD])
            we = jnp.exp2(scores * EXP2_SCALE) * mask[m]
            wexp[i, u] = we
            part = we[:, :HD] + we[:, HD:]
            val = dot(we.astype(BF), kv[t, :, HD:])
            if first:
                den[u] = part
                num[u] = val
            else:
                den[u] += part
                num[u] += val

    def loop2(fn):
        lax.fori_loop(0, 2, lambda i, carry: (fn(i), carry)[1], 0)

    def grad_att(j, acc):
        cols = pl.ds(pl.multiple_of(j * 384, 384), 384)
        return acc + dot(cot[:, cols], wo[pl.ds(2 * j, 2)].reshape(2 * OWN, WID))

    def two(first, second):
        forward(*first)
        forward(*second)

    def side(zz, i):
        two((at_tile(zz, p.xl, 1 - p.c), 2, 4 + 2 * i), (at_tile(zz, p.xr, 1 - p.c), 2, 5 + 2 * i))

    forward(p.me, 0, 0, (0, 2), True)
    gather_o.step_sides_across()
    gather_ka.step_across()
    gather_kb.step_across()
    gather_o.step_opposite()
    gather_ka.sib_own()
    gather_kb.sib_own()
    q_pair.wait_recv()
    qt[1] = q[1].T
    forward(p.me, 0, 0, (1,), True)
    forward(p.sib, 1, 2)
    gather_kb.step_sides()
    gather_ka.step_sides()
    gather_ka.step_sides_across()
    gather_kb.step_sides_across()
    forward(p.across, 0, 1)
    gather_o.step_last()
    gather_ka.sib_sides()
    gather_kb.sib_sides()
    side(p.z, 0)
    gather_ka.step_opposite()
    gather_kb.step_opposite()
    gather_ka.sib_across()
    gather_kb.sib_across()
    two((at_tile(1 - p.z, p.x, 1 - p.c), 1, 3), (at_tile(p.z, p.xo, p.c), 0, 8))
    gather_o.sib_own()
    gather_o.sib_across()
    gather_o.sib_sides()
    gather_o.sib_sides_across()
    gather_o.sib_opposite()
    gather_o.sib_last()
    g_all[...] = lax.fori_loop(0, 8, grad_att, jnp.zeros((ROWS, WID), F32)).astype(BF)
    pair_out[1] = of_x(lambda cols: g_all[:, cols])
    g_pair = to_across(1, g.at[1])
    gather_ka.step_last()
    gather_kb.step_last()
    gather_ka.sib_sides_across()
    gather_kb.sib_sides_across()
    side(1 - p.z, 1)
    g[0] = of_a(lambda cols: g_all[:, cols])
    g[2] = of_b(lambda cols: g_all[:, cols])
    for u in (0, 2):
        gt[u] = g[u].T
    gather_ka.sib_opposite()
    gather_kb.sib_opposite()
    two((at_tile(p.z, p.xo, 1 - p.c), 1, 10), (at_tile(1 - p.z, p.xo, p.c), 0, 9))
    gather_ka.sib_last()
    gather_kb.sib_last()
    forward(at_tile(1 - p.z, p.xo, 1 - p.c), 1, 11)
    g_pair.wait_recv()
    gt[1] = g[1].T

    for u in (1, 0, 2):
        inverse = 1.0 / jnp.sum(den[u], axis=-1, keepdims=True)
        context = num[u] * inverse
        if u == 1:
            pair_out[2] = context.astype(BF)
            att_pair = to_across(2, pair_in.at[0])
        else:
            att[0, head_a if u == 0 else 1] = context.astype(BF)
        row = jnp.sum(g[u].astype(F32) * context, axis=-1, keepdims=True)
        delta[u] = jnp.broadcast_to(row, (ROWS, HD))
        den[u] = jnp.broadcast_to(inverse, (ROWS, HD))

    def backward(t, i, x, z, own):
        block(backward_block, t, i, x, z, own)

    def backward_block(t, i, x, z, own):
        dk, dv = [], []
        for u in range(NH):
            kv = kva if u < 2 else kvb
            grad = dot_nt(g[u], kv[t, :, HD:])
            inverse, row = den[u], delta[u]
            probs, ds = [], []
            for part in range(2):
                cs = slice(part * HD, (part + 1) * HD)
                pr = wexp[i, u, :, cs] * inverse
                ds.append((pr * (grad[:, cs] - row)).astype(BF))
                probs.append(pr.astype(BF))
            probs = jnp.concatenate(probs, axis=1)
            ds = jnp.concatenate(ds, axis=1)
            dq[u] += dot(ds, kv[t, :, :HD])
            dk.append(dot(qt[u], ds))
            dv.append(dot(gt[u], probs))
        for n, ks, vs in ((0, dk[0] + dk[1], dv[0] + dv[1]), (1, dk[2], dv[2])):
            ks = ks * INV_ROOT
            if own:
                ks = ks + d_parts[n, x, z, :HD].astype(F32)
                vs = vs + d_parts[n, x, z, HD:].astype(F32)
            out = d_parts if own else d_out
            out[n, x, z, :HD] = ks.astype(BF)
            out[n, x, z, HD:] = vs.astype(BF)

    def swap_copy(x, z, k):
        return pltpu.make_async_remote_copy(
            src_ref=d_out.at[:, x, z], dst_ref=d_parts.at[:, x, z], send_sem=dkv_send.at[k], recv_sem=dkv_recv.at[k],
            device_id={"tile": p.sib}, device_id_type=MESH)

    def swap(x, z, k):
        c = swap_copy(x, z, k)
        c.start()
        sent.append(c)

    def swapped(x, z, k):
        swap_copy(x, z, k).wait_recv()

    def out_part(ring):
        def one(i):
            o = wo[pl.ds(4 * ring + 2 * i, 2)].reshape(2 * OWN, WID)
            ho_parts[ring, i] = dot_nt(wide(att, 0), o).astype(BF)
        loop2(one)

    def tok_part(ring):
        def one(i):
            j = 2 * ring + i
            acc = dot_nt(wide(gp, 0, 0), w[pl.ds(2 * j, 2), 0:OWN, :].reshape(2 * OWN, WID))
            for n in range(1, 3):
                acc += dot_nt(wide(gp, 0, n), w[pl.ds(2 * j, 2), n * OWN:(n + 1) * OWN, :].reshape(2 * OWN, WID))
            ht_parts[ring, i] = acc.astype(BF)
        loop2(one)

    def out_grad(ring):
        def one(i):
            j = 4 * i + ring
            go_parts[ring, i] = (dot(cot_t[j, p.c], wide(att, 0)) + dot(cot_sib[j], wide(att, 1))).astype(BF)
        loop2(one)

    def qkv_grad(parts, j, which):
        for n, i in enumerate(which):
            parts[j % 4, j // 4, n * OWN:(n + 1) * OWN] = (
                dot(tok_t[j, p.c], wide(gp, 0, i)) + dot(tok_sib[j], wide(gp, 1, i))).astype(BF)

    def kv_grad(ring):
        loop2(lambda i: qkv_grad(gk_parts, i * 4 + ring, (1, 2)))

    def opposite_sib(i):
        zz = (p.z + i) % 2
        backward(at_tile(zz, p.xo, 1 - p.c), 10 + i, 2, i, False)

    def opposite_own(i):
        zz = (p.z + i) % 2
        backward(at_tile(zz, p.xo, p.c), 8 + i, 2, i, True)

    def sides_sib(i):
        zz = (p.z + 1 + i) % 2
        backward(at_tile(zz, p.xl, 1 - p.c), 6 - 2 * i, 3, 1 - i, False)
        backward(at_tile(zz, p.xr, 1 - p.c), 7 - 2 * i, 1, 1 - i, False)

    def own_sib(i):
        zz = (p.z + i) % 2
        backward(at_tile(zz, p.x, 1 - p.c), 2 + i, 0, i, False)

    def own_own(i):
        zz = (p.z + i) % 2
        backward(at_tile(zz, p.x, p.c), i, 0, i, True)

    def unit_back(grad, raw):
        scale = scale_of(raw)
        unit = raw * scale
        return scale * (grad - unit * jnp.mean(grad * unit, axis=-1, keepdims=True))

    dq[...] = jnp.zeros_like(dq)
    opposite_sib(1)
    swap(2, 1, 0)
    opposite_sib(0)
    swap(2, 0, 1)
    swapped(2, 1, 0)
    opposite_own(1)
    sum_da.start_far(0)
    sum_db.start_far(0)
    swapped(2, 0, 1)
    opposite_own(0)
    sum_da.start_far(1)
    sum_db.start_far(1)
    att_pair.wait_recv()
    att[0, head_x] = pair_in[0]
    att_swap = to_sibling(2, att.at[0], att.at[1])
    sides_sib(0)
    swap(3, 1, 2)
    swap(1, 1, 3)
    cot_swap.wait_recv()
    att_swap.wait_recv()
    out_grad(p.xo)
    sum_go.start_far(0, False)
    sum_go.start_far(1, False)
    sides_sib(1)
    swap(3, 0, 4)
    swap(1, 0, 5)
    out_part(sum_out.ro)
    sum_out.start_far(0)
    sum_out.start_far(1)
    swapped(3, 1, 2)
    swapped(1, 1, 3)
    sum_da.start_near(0)
    sum_db.start_near(0)
    out_part(sum_out.rr)
    out_part(sum_out.rl)
    sum_out.start_near(0)
    sum_out.start_near(1)
    swapped(3, 0, 4)
    swapped(1, 0, 5)
    sum_da.start_near(1)
    sum_db.start_near(1)
    sum_da.step_near(0)
    sum_db.step_far_b()
    out_grad(p.xr)
    out_grad(p.xl)
    sum_go.start_z(0, p.xo)
    sum_go.start_z(1, p.xr)
    sum_go.start_z(2, p.xl)
    loop2(own_sib)
    swap(0, 0, 6)
    swap(0, 1, 7)
    sum_db.step_near(0)
    sum_da.step_near(1)
    sum_db.step_near(1)
    swapped(0, 0, 6)
    swapped(0, 1, 7)
    loop2(own_own)
    sum_db.start_own()
    pair_out[3] = dq[1].astype(BF)
    dq_pair = to_across(3, pair_in.at[1])
    out_grad(p.x)
    sum_db.step_near_b()
    sum_go.start_near(0, False)
    sum_go.start_near(1, False)
    sum_go.step_near(0)
    sum_go.step_near(1)
    sum_go.start_own()
    out_part(sum_out.ring)
    sum_da.step_pair()
    sum_db.step_pair()

    def head_grad(i, of, head, grad):
        gp[0, i, head] = unit_back(grad, head_of(of, i)).astype(BF)

    head_grad(0, of_a, head_a, dq[0] * INV_ROOT)
    head_grad(0, of_b, 1, dq[2] * INV_ROOT)
    dq_pair.wait_recv()
    head_grad(0, of_x, head_x, pair_in[1].astype(F32) * INV_ROOT)
    gq_swap = to_sibling(3, gp.at[0, 0], gp.at[1, 0])
    sum_out.step_near(0)
    sum_out.step_near(1)

    tok_swap.wait_recv()
    gq_swap.wait_recv()
    lax.fori_loop(0, 8, lambda j, carry: (qkv_grad(gq_parts, j, (0,)), carry)[1], 0)
    gather_w.finish()
    gather_o.finish()
    sum_gq.start_far(0, False)
    sum_gq.start_far(1, False)
    sum_gq.start_near(0, False)
    sum_gq.start_near(1, False)
    sum_gq.start_over()

    def kv_head(n, of, head):
        head_grad(1, of, head, dkv_sum[n, :HD].T)
        gp[0, 2, head] = dkv_sum[n, HD:].T.astype(BF)

    sum_da.result_own(dkv_sum.at[0])
    kv_head(0, of_a, head_a)
    sum_db.result_b(dkv_sum.at[1])
    sum_db.result_a(dkv_sum.at[1])
    kv_head(1, of_b, 1)
    sum_da.result_last(dkv_sum.at[2])
    kv_head(2, of_x, head_x)
    gk_swap = to_sibling(4, gp.at[0, pl.ds(1, 2)], gp.at[1, pl.ds(1, 2)])

    sum_out.step_pair()
    sum_go.step_far_b()
    tok_part(sum_tok.ro)
    sum_tok.start_far(0)
    sum_tok.start_far(1)
    gk_swap.wait_recv()
    kv_grad(p.xo)
    sum_gk.start_far(0)
    sum_gk.start_far(1)
    sum_go.step_pair()
    sum_gq.step_near(0)
    sum_gq.step_near(1)
    sum_go.step_near_b()
    tok_part(sum_tok.rr)
    tok_part(sum_tok.rl)
    sum_tok.start_near(0)
    sum_tok.start_near(1)
    kv_grad(p.xr)
    kv_grad(p.xl)
    sum_gk.start_near(0)
    sum_gk.start_near(1)
    sum_gq.step_far_b()
    tok_part(sum_tok.ring)
    sum_tok.step_near(0)
    sum_tok.step_near(1)
    kv_grad(p.x)
    sum_gk.start_own()
    sum_gk.step_near(0)
    sum_gk.step_near(1)
    sum_gk.step_far_b()
    sum_gq.step_near_b()
    sum_out.result_a(out_ref)
    sum_go.result_b(gout_ref)
    sum_go.result_a(gout_ref)
    sum_tok.step_pair()
    sum_gq.step_pair()
    sum_gk.step_near_b()
    sum_gk.step_pair()
    sum_gq.result_b(gqkv_ref.at[pl.ds(0, OWN)])
    sum_gq.result_a(gqkv_ref.at[pl.ds(0, OWN)])
    sum_tok.result_a(gtok_ref)
    sum_gk.result_b(gqkv_ref.at[pl.ds(OWN, 2 * OWN)])
    sum_gk.result_a(gqkv_ref.at[pl.ds(OWN, 2 * OWN)])

    for s in (gather_ka, gather_kb, sum_da, sum_db, sum_gq, sum_gk, sum_go, sum_out, sum_tok):
        s.finish()
    for c in sent:
        c.wait_send()


def lane_bufs(rows, first, cols):
    _, ah, _, bh = split_rows(rows, first)
    second = rows - first
    bufs = [(2, 2, ah[0].size, cols), (2, 2, first, cols), (first, cols)]
    if second:
        bufs += [(4, second, cols), (2, bh[1].size, cols), (2, second, cols)]
    return [pltpu.VMEM(b, BF) for b in bufs]


def deliver(*refs):
    for i in range(4):
        refs[4 + i][...] = refs[i][...]


def local(tokens, cotangent, qkv_weight, out_weight, slab_of_device, extents):
    w = jnp.transpose(qkv_weight, (1, 0, 2)).reshape(3 * OWN, WID)
    vm = lambda *shape, dtype=BF: pltpu.VMEM(shape, dtype)
    dma = lambda *shape: pltpu.SemaphoreType.DMA(shape)
    scratch = [
        vm(16, 3 * OWN, WID), vm(16, OWN, WID), vm(16, ROWS, ROWS), vm(16, ROWS, ROWS), vm(ROWS, ROWS), vm(ROWS, D), vm(ROWS, D),
        vm(8, 2, OWN, ROWS), vm(8, OWN, ROWS), vm(8, 2, OWN, ROWS), vm(8, OWN, ROWS),
        vm(12, NH, ROWS, ROWS, dtype=F32), vm(3, ROWS, ROWS, dtype=F32),
        vm(3, ROWS, WID, dtype=F32), vm(NH, ROWS, HD), vm(NH, HD, ROWS),
        vm(ROWS, WID), vm(NH, ROWS, HD), vm(NH, HD, ROWS),
        vm(NH, ROWS, HD, dtype=F32), vm(NH, ROWS, HD, dtype=F32), vm(NH, ROWS, HD, dtype=F32),
        vm(NH, ROWS, HD, dtype=F32), vm(2, NH, ROWS, HD), vm(2, 3, NH, ROWS, HD), vm(NH, ROWS, ROWS, dtype=F32),
        vm(4, ROWS, HD), vm(2, ROWS, HD),
        vm(2, 4, 2, ROWS, ROWS), vm(2, 4, 2, ROWS, ROWS),
        *lane_bufs(ROWS, ROWS, ROWS), *lane_bufs(ROWS, DKV_FIRST, ROWS),
        vm(4, 2, OWN, WID), *lane_bufs(OWN, SUM_FIRST, WID),
        vm(4, 2, 2 * OWN, WID), *lane_bufs(2 * OWN, KVW_FIRST, WID),
        vm(4, 2, OWN, WID), *lane_bufs(OWN, SUM_FIRST, WID),
        vm(4, 2, ROWS, WID), *lane_bufs(ROWS, ROWS, WID), vm(4, 2, ROWS, WID), *lane_bufs(ROWS, ROWS, WID),
        dma(4), dma(SEMS), dma(SEMS), dma(5), dma(5), dma(8), dma(8), dma(4), dma(4),
    ]
    any_spec = pl.BlockSpec(memory_space=pl.ANY)
    smem = pl.BlockSpec(memory_space=pltpu.SMEM)
    vmem = pl.BlockSpec(memory_space=pltpu.VMEM)
    shapes = (
        jax.ShapeDtypeStruct((ROWS, WID), BF), jax.ShapeDtypeStruct((ROWS, WID), BF),
        jax.ShapeDtypeStruct((3 * OWN, WID), F32), jax.ShapeDtypeStruct((OWN, WID), F32))
    results = pl.pallas_call(
        kernel,
        out_shape=shapes,
        in_specs=[any_spec] * 4 + [smem] * 2,
        out_specs=(vmem,) * 4,
        scratch_shapes=scratch,
        compiler_params=pltpu.CompilerParams(
            collective_id=0, has_side_effects=True, vmem_limit_bytes=64 * 1024 * 1024),
        cost_estimate=pl.CostEstimate(flops=20_000_000_000, bytes_accessed=10_000_000, transcendentals=2_400_000),
        name="sublayer",
    )(tokens, cotangent, w, out_weight, slab_of_device, extents.T)
    output, grad_tokens, grad_qkv, grad_out = pl.pallas_call(
        deliver, out_shape=shapes, in_specs=[vmem] * 4, out_specs=(vmem,) * 4, name="deliver")(*results)
    grad_qkv = jnp.transpose(grad_qkv.reshape(3, OWN, WID), (1, 0, 2))
    return output, grad_tokens, grad_qkv, grad_out


def solution(mesh):
    return jax.shard_map(
        local, mesh=mesh,
        in_specs=(P("tile", None), P("tile", None), P("tile", None, "head"), P("tile", "head"), P(None), P(None, None)),
        out_specs=(P("tile", "head"), P("tile", "head"), P("tile", None, "head"), P("tile", "head")),
        check_vma=False)
```
